32 devices in a mesh: arrays: 2 (over y), tm: 8 (over z, x), chan: 2 (over core).
Axes of the slice: x: 2, y: 2, z: 4, core: 2. Of those that a mesh axis runs over, the one named last changes fastest.
Arguments:
- spectra: bfloat16 [128, 256, 2, 128], P(('arrays', 'tm'), 'chan'), parts along dimension 0, may hold values from -40 to 40
- offsets: int32 [128], P(('arrays', 'tm')), parts along dimension 0, may hold values from 0 to 63
- channel_group: int32 [512], P(('arrays', 'chan')), parts along dimension 0, may hold values from 0 to 7
Outputs:
- stack: float32 [128, 48, 128], P(('arrays', 'tm', 'chan')), parts along dimension 0
The draws below stay inside these ranges and needn't reach their ends.
There are 2 independent parts, one for each index of `arrays`. The reference program is written for one: setup_inputs(seed, part) draws one part's arguments, and reference() takes and returns one part's arrays. A program takes and returns all parts, laid end to end along the dimension named above; each array names one. Nothing has to cross between parts.
All inputs are finite; a program needn't handle non-finite values.
Results may differ from the reference program's by a relative error of at most 0.0075.
Values may be sent and summed in bfloat16 or wider, within the bound.
No kernel may reach another device: no remote copies, remote signals or barrier semaphores. Data moves between devices by JAX's collectives and lax.ppermute only.
A program may use at most 64 MiB of HBM per device.

```python
import math
import jax
import jax.numpy as jnp
from jax import lax

F = 128
LAGS = 128
GROUPS = 8
BAND = 48
WINDOWS = 64
CHANNELS = 256


def draw_spectra(key, part):
    key_amplitude = jax.random.fold_in(key, 11)
    key_values = jax.random.fold_in(key, 12)
    amplitude = jnp.exp(jax.random.uniform(key_amplitude, (WINDOWS, CHANNELS, 1, 1), jnp.float32, math.log(0.1), math.log(10.0)))
    values = jnp.clip(jax.random.normal(key_values, (WINDOWS, CHANNELS, 2, F), jnp.float32), -4.0, 4.0)
    return (amplitude * values).astype(jnp.bfloat16)


def plant(result, key, low, high):
    longest = result.shape.index(max(result.shape))
    spots = []
    for shift in (0, 1):
        where = [jax.random.randint(jax.random.fold_in(key, axis), (), 0, length) for axis, length in enumerate(result.shape)]
        where[longest] = (where[longest] + shift) % result.shape[longest]
        spots.append(tuple(where))
    return result.at[spots[0]].set(low).at[spots[1]].set(high)


def setup_inputs(seed: int = 0, part: int = 0) -> dict:
    key_of = jax.random.split(jax.random.key(seed), 4)
    part_splits = jax.random.split(jax.random.fold_in(key_of[3], part), 4)
    return {
        "spectra": draw_spectra(jax.random.fold_in(jax.random.fold_in(key_of[3], part), 71), part),
        "offsets": plant(jax.random.randint(part_splits[1], (WINDOWS,), 0, LAGS // 2), jax.random.fold_in(part_splits[1], 1), 0, (LAGS // 2) - 1).astype(jnp.int32),
        "channel_group": plant(jax.random.randint(part_splits[2], (CHANNELS,), 0, GROUPS), jax.random.fold_in(part_splits[2], 1), 0, GROUPS - 1).astype(jnp.int32),
    }


epsilon = 1e-05

def lag_table(freq_bins, lag_count):
    frequency = jnp.arange(freq_bins, dtype=jnp.int32)[:, None]
    lag_shift = jnp.arange(lag_count, dtype=jnp.int32)[None, :] - lag_count // 2
    phase_turns = jnp.mod(frequency * lag_shift, 2 * freq_bins).astype(jnp.float32)
    phase_angle = jnp.pi * phase_turns / freq_bins
    normaliser = 1.0 / math.sqrt(freq_bins)
    lag_rows = jnp.concatenate([jnp.cos(phase_angle) * normaliser, -jnp.sin(phase_angle) * normaliser], axis=0)
    return lag_rows.astype(jnp.bfloat16)

def align_spectra(spectra, offsets, scales):
    freq_bins = spectra.shape[3]
    frequency = jnp.arange(freq_bins, dtype=jnp.int32)[None, :]
    phase_turns = jnp.mod(offsets[:, None] * frequency, 2 * freq_bins).astype(jnp.float32)
    phase_angle = jnp.pi * phase_turns / freq_bins
    cosine = jnp.cos(phase_angle)[:, None, :]
    sine_part = jnp.sin(phase_angle)[:, None, :]
    real_part = spectra[:, :, 0, :].astype(jnp.float32)
    imag_part = spectra[:, :, 1, :].astype(jnp.float32)
    weight = scales[:, :, None]
    out_real = weight * (real_part * cosine + imag_part * sine_part)
    out_imag = weight * (imag_part * cosine - real_part * sine_part)
    return jnp.stack([out_real, out_imag], axis=2).astype(jnp.bfloat16)

def window_terms(current, band_rows, lag_rows):
    left_real = current[None, :, 0, :].astype(jnp.float32)
    left_imag = current[None, :, 1, :].astype(jnp.float32)
    right_real = band_rows[:, :, 0, :].astype(jnp.float32)
    right_imag = band_rows[:, :, 1, :].astype(jnp.float32)
    prod_real = left_real * right_real + left_imag * right_imag
    prod_imag = left_imag * right_real - left_real * right_imag
    cross_spec = jnp.stack([prod_real, prod_imag], axis=2).astype(jnp.bfloat16)
    flattened = cross_spec.reshape(band_rows.shape[0] * band_rows.shape[1], 2 * band_rows.shape[3])
    lagged = jnp.dot(flattened.astype(jnp.float32), lag_rows.astype(jnp.float32), precision=lax.Precision.HIGHEST)
    lagged = lagged.reshape(band_rows.shape[0], band_rows.shape[1], lag_rows.shape[1])
    return lax.optimization_barrier(jnp.sum(lagged * lagged, axis=1))

def reference(spectra, offsets, channel_group):
    chan_power = lax.optimization_barrier(jnp.sum(jnp.square(spectra.astype(jnp.float32)), axis=(2, 3)))
    onehot = (channel_group[:, None] == jnp.arange(GROUPS, dtype=jnp.int32)[None, :]).astype(jnp.float32)
    group_total = jnp.dot(chan_power, onehot, precision=lax.Precision.HIGHEST)
    energy = group_total * (GROUPS / (F * CHANNELS))
    scales = jnp.dot(lax.rsqrt(energy + epsilon), onehot.T, precision=lax.Precision.HIGHEST)
    aligned = align_spectra(spectra, offsets, scales)
    padded = jnp.concatenate([jnp.zeros((BAND, CHANNELS, 2, F), jnp.bfloat16), aligned], axis=0)
    lag_rows = lag_table(F, LAGS)

    def one_window(window):
        current = lax.dynamic_index_in_dim(aligned, window, 0, keepdims=False)
        band_rows = lax.dynamic_slice_in_dim(padded, window, BAND, 0)
        return window_terms(current, band_rows, lag_rows)
    summed = lax.map(one_window, jnp.arange(WINDOWS, dtype=jnp.int32))
    return summed * (1.0 / CHANNELS)
```

```python
import functools
import math

import jax
import jax.numpy as jnp
from jax import lax
from jax.experimental import pallas as pl
from jax.experimental.pallas import tpu as pltpu
from jax.sharding import PartitionSpec as P

LAGS = 128
GROUPS = 8
SPAN = 6
SIDES = 2
LEVELS = 4
TEAM = SIDES * LEVELS

epsilon = 1e-05

HIGHEST = lax.Precision.HIGHEST


def lag_table(freq_bins, lag_count):
    frequency = jnp.arange(freq_bins, dtype=jnp.int32)[:, None]
    lag_shift = jnp.arange(lag_count, dtype=jnp.int32)[None, :] - lag_count // 2
    phase_turns = jnp.mod(frequency * lag_shift, 2 * freq_bins).astype(jnp.float32)
    phase_angle = jnp.pi * phase_turns / freq_bins
    normaliser = 1.0 / math.sqrt(freq_bins)
    lag_rows = jnp.concatenate(
        [jnp.cos(phase_angle) * normaliser, -jnp.sin(phase_angle) * normaliser], axis=0
    )
    return lag_rows.astype(jnp.bfloat16)


def phases(offsets, freq_bins):
    frequency = jnp.arange(freq_bins, dtype=jnp.int32)[None, :]
    phase_turns = jnp.mod(offsets[:, None] * frequency, 2 * freq_bins).astype(jnp.float32)
    phase_angle = jnp.pi * phase_turns / freq_bins
    return jnp.stack([jnp.cos(phase_angle), jnp.sin(phase_angle)])


def member_rows(group_row):
    channels = group_row.shape[1]
    groups = lax.broadcasted_iota(jnp.int32, (GROUPS, channels), 0)
    return (group_row == groups).astype(jnp.float32)


def power_kernel(spectra_ref, group_ref, power_ref, rows_ref):
    windows, rows, _ = spectra_ref.shape
    member = member_rows(group_ref[...])
    lane = lax.broadcasted_iota(jnp.int32, power_ref.shape, 1)
    power = jnp.zeros(power_ref.shape, jnp.float32)
    for window in range(windows):
        value = spectra_ref[window].astype(jnp.float32)
        rows_ref[window] = value * value
        squares = rows_ref[window, pl.ds(0, rows // 2, stride=2), :] + rows_ref[window, pl.ds(1, rows // 2, stride=2), :]
        grouped = jnp.dot(member, squares, precision=HIGHEST, preferred_element_type=jnp.float32)
        power = jnp.where(lane == window, jnp.sum(grouped, axis=1, keepdims=True), power)
    power_ref[...] = power


def align_kernel(scale_of_energy, spectra_ref, group_ref, own_ref, other_ref, phase_ref, *rest):
    pieces, (rows_ref, scale_ref) = rest[:LEVELS], rest[LEVELS:]
    windows, rows, _ = spectra_ref.shape
    part = rows // 2 // LEVELS
    level = lax.rem(lax.axis_index("tm"), TEAM) // SIDES
    energy = (own_ref[...] + other_ref[...]) * scale_of_energy
    scale_ref[...] = lax.dot_general(
        member_rows(group_ref[...]), lax.rsqrt(energy + epsilon), (((0,), (0,)), ((), ())),
        precision=HIGHEST, preferred_element_type=jnp.float32,
    )
    for window in range(windows):
        rows_ref[window] = spectra_ref[window].astype(jnp.float32)
    for step in range(LEVELS):
        first = pl.multiple_of((level ^ step) * part, part)
        weights = scale_ref[pl.ds(first, part), :]
        for window in range(windows):
            cosine = phase_ref[0, window : window + 1, :]
            sine = phase_ref[1, window : window + 1, :]
            real = rows_ref[window, pl.ds(2 * first, part, stride=2), :]
            imag = rows_ref[window, pl.ds(2 * first + 1, part, stride=2), :]
            weight = weights[:, window : window + 1]
            pieces[step][window, 0] = (weight * (real * cosine + imag * sine)).astype(jnp.bfloat16)
            pieces[step][window, 1] = (weight * (imag * cosine - real * sine)).astype(jnp.bfloat16)


def stack_kernel(blocks_before, count, *refs):
    table_ref = refs[0]
    pieces = refs[1 : 1 + count]
    outs = refs[1 + count : 1 + count + LEVELS]
    held, sems = refs[1 + count + LEVELS :]
    windows, _, part, _ = pieces[0].shape
    member = lax.rem(lax.axis_index("tm"), TEAM)
    side, level = lax.rem(member, SIDES), member // SIDES
    core = lax.axis_index("chan")
    halves = held.shape[2] // part
    copies = []
    for index, piece in enumerate(pieces):
        slot, half = index // halves, index % halves
        round_, slot = slot // TEAM, slot % TEAM
        hop, step = slot // LEVELS, slot % LEVELS
        block = (level ^ step) * SIDES + (side ^ hop)
        place = (block + (blocks_before if round_ == 0 else 0)) * windows
        copies.append(pltpu.make_async_copy(
            piece, held.at[pl.ds(place, windows), :, pl.ds(half * part, part), :], sems.at[index]))
    for copy in copies:
        copy.start()
    if count == TEAM * halves:
        held[pl.ds(0, blocks_before * windows)] = jnp.zeros((blocks_before * windows,) + held.shape[1:], held.dtype)
    for copy in copies:
        copy.wait()
    table = table_ref[...]
    batch = windows
    channels, freq = held.shape[2], held.shape[3]
    band = outs[0].shape[1]
    keep = outs[0].shape[0]
    for step in range(LEVELS):
        out = outs[step]
        block = (level ^ step) * SIDES + side + blocks_before
        for inner in range(keep):
            window = block * windows + core * keep + inner
            lowest = jnp.maximum(0, (band - window) // batch)
            if count == TEAM * halves:
                lowest = jnp.maximum(0, (band + (blocks_before * windows) - window) // batch)

            def clear(index, carry):
                out[inner, pl.ds(pl.multiple_of(index * batch, batch), batch), :] = jnp.zeros((batch, out.shape[2]), out.dtype)
                return carry

            def one(index, carry):
                start = window - band + index * batch
                left_real = held[window, 0][None]
                left_imag = held[window, 1][None]
                right_real = held[pl.ds(start, batch), 0]
                right_imag = held[pl.ds(start, batch), 1]
                real = left_real * right_real + left_imag * right_imag
                imag = left_imag * right_real - left_real * right_imag
                cross = jnp.concatenate(
                    [real.reshape(batch * channels, freq), imag.reshape(batch * channels, freq)], axis=1)
                lagged = jnp.dot(cross, table, preferred_element_type=jnp.float32)
                total = jnp.sum((lagged * lagged).reshape(batch, channels, table.shape[1]), axis=1)
                out[inner, pl.ds(pl.multiple_of(index * batch, batch), batch), :] = total.astype(out.dtype)
                return carry

            lax.fori_loop(0, lowest, clear, 0)
            lax.fori_loop(lowest, band // batch, one, 0)


def vmem():
    return pl.BlockSpec(memory_space=pltpu.VMEM)


def flip(value, axis, size, bits):
    return lax.ppermute(value, axis, [(source, source ^ bits) for source in range(size)])


def shards(spectra, offsets, channel_group):
    windows, local_chans, _, freq = spectra.shape
    chan_count = lax.axis_size("chan")
    tm_count = lax.axis_size("tm")
    channels = local_chans * chan_count
    part = local_chans // LEVELS
    band = SPAN * windows
    keep = windows // chan_count
    params = pltpu.CompilerParams(vmem_limit_bytes=48 * 1024 * 1024)

    rows = spectra.reshape(windows, 2 * local_chans, freq)
    group_row = channel_group.reshape(1, local_chans)
    power = pl.pallas_call(
        power_kernel,
        out_shape=jax.ShapeDtypeStruct((GROUPS, 128), jnp.float32),
        in_specs=[vmem(), vmem()],
        out_specs=vmem(),
        scratch_shapes=[pltpu.VMEM((windows, 2 * local_chans, freq), jnp.float32)],
        compiler_params=params,
        name="power",
    )(rows, group_row)
    other_power = flip(power, "chan", chan_count, 1)
    piece_shape = jax.ShapeDtypeStruct((windows, 2, part, freq), jnp.bfloat16)
    own = pl.pallas_call(
        functools.partial(align_kernel, GROUPS / (freq * channels)),
        out_shape=[piece_shape] * LEVELS,
        in_specs=[vmem()] * 5,
        out_specs=[vmem()] * LEVELS,
        scratch_shapes=[
            pltpu.VMEM((windows, 2 * local_chans, freq), jnp.float32),
            pltpu.VMEM((local_chans, 128), jnp.float32),
        ],
        compiler_params=params,
        name="align",
    )(rows, group_row, power, other_power, phases(offsets, freq))

    near = [own[0]] + [None] * (LEVELS - 1)
    far = [None] * LEVELS
    order = (2, 1, 3)
    near[2] = flip(own[2], "tm", tm_count, 2 * SIDES)
    far[0] = flip(own[0], "tm", tm_count, 1)
    near[1] = flip(own[1], "tm", tm_count, 1 * SIDES)
    near[3] = flip(own[3], "tm", tm_count, 3 * SIDES)
    for step in order:
        far[step] = flip(near[step], "tm", tm_count, 1)
    held = []
    for piece in near + far:
        held += [piece, flip(piece, "chan", chan_count, 1)]
    before = 1
    if tm_count > TEAM:
        pairs = [(source, source + TEAM) for source in range(tm_count - TEAM)]
        held += [lax.ppermute(piece, "tm", pairs) for piece in held]
        before = TEAM
    count = len(held)

    sums = pl.pallas_call(
        functools.partial(stack_kernel, before, count),
        out_shape=[
            jax.ShapeDtypeStruct((keep, band, LAGS), jnp.float32 if step == 0 else jnp.bfloat16) for step in range(LEVELS)
        ],
        in_specs=[vmem()] + [pl.BlockSpec(memory_space=pl.ANY)] * count,
        out_specs=[vmem()] * LEVELS,
        scratch_shapes=[
            pltpu.VMEM(((before + TEAM) * windows, 2, part * chan_count, freq), jnp.bfloat16),
            pltpu.SemaphoreType.DMA((count,)),
        ],
        compiler_params=params,
        name="stack",
    )(lag_table(freq, LAGS), *held)
    total = sums[0]
    for step in range(1, LEVELS):
        total = total + flip(sums[step], "tm", tm_count, step * SIDES).astype(jnp.float32)
    return total * (1.0 / channels)


def solution(mesh):
    placed = (P(("arrays", "tm"), "chan", None, None), P(("arrays", "tm")), P(("arrays", "chan")))
    return jax.shard_map(
        shards,
        mesh=mesh,
        in_specs=placed,
        out_specs=P(("arrays", "tm", "chan"), None, None),
        check_vma=False,
    )
```

```python
import functools
import math

import jax
import jax.numpy as jnp
from jax import lax
from jax.experimental import pallas as pl
from jax.experimental.pallas import tpu as pltpu
from jax.sharding import PartitionSpec as P

LAGS = 128
GROUPS = 8
SPAN = 6
SIDES = 2
LEVELS = 4
TEAM = SIDES * LEVELS
EARLY = (("near", 2), ("far", 0), ("near", 3), ("near", 1), ("far", 1))
LATE = (2, 3)
OUT_ORDER = (2, 3, 1)

epsilon = 1e-05

HIGHEST = lax.Precision.HIGHEST


def lag_table(freq_bins, lag_count):
    frequency = jnp.arange(freq_bins, dtype=jnp.int32)[:, None]
    lag_shift = jnp.arange(lag_count, dtype=jnp.int32)[None, :] - lag_count // 2
    phase_turns = jnp.mod(frequency * lag_shift, 2 * freq_bins).astype(jnp.float32)
    phase_angle = jnp.pi * phase_turns / freq_bins
    normaliser = 1.0 / math.sqrt(freq_bins)
    lag_rows = jnp.concatenate(
        [jnp.cos(phase_angle) * normaliser, -jnp.sin(phase_angle) * normaliser], axis=0
    )
    return lag_rows.astype(jnp.bfloat16)


def phases(offsets, freq_bins):
    frequency = jnp.arange(freq_bins, dtype=jnp.int32)[None, :]
    phase_turns = jnp.mod(offsets[:, None] * frequency, 2 * freq_bins).astype(jnp.float32)
    phase_angle = jnp.pi * phase_turns / freq_bins
    return jnp.stack([jnp.cos(phase_angle), jnp.sin(phase_angle)])


def power_kernel(spectra_ref, member_ref, power_ref, rows_ref):
    windows, rows, _ = spectra_ref.shape
    half = rows // 2
    lane = lax.broadcasted_iota(jnp.int32, power_ref.shape, 1)
    power = jnp.zeros(power_ref.shape, jnp.float32)
    for window in range(windows):
        value = spectra_ref[window].astype(jnp.float32)
        rows_ref[window] = value * value
        squares = rows_ref[window, pl.ds(0, half, stride=2), :] + rows_ref[window, pl.ds(1, half, stride=2), :]
        grouped = jnp.dot(member_ref[...], squares, precision=HIGHEST, preferred_element_type=jnp.float32)
        power = jnp.where(lane == window, jnp.sum(grouped, axis=1, keepdims=True), power)
    power_ref[...] = power


def align_kernel(scale_of_energy, spectra_ref, member_ref, own_ref, other_ref, phase_ref, *rest):
    pieces, (rows_ref, scale_ref) = rest[:LEVELS], rest[LEVELS:]
    windows, rows, _ = spectra_ref.shape
    part = rows // 2 // LEVELS
    level = lax.rem(lax.axis_index("tm"), TEAM) // SIDES
    energy = (own_ref[...] + other_ref[...]) * scale_of_energy
    scale_ref[...] = lax.dot_general(
        member_ref[...], lax.rsqrt(energy + epsilon), (((0,), (0,)), ((), ())),
        precision=HIGHEST, preferred_element_type=jnp.float32,
    )
    for window in range(windows):
        rows_ref[window] = spectra_ref[window].astype(jnp.float32)
    for step in range(LEVELS):
        first = pl.multiple_of((level ^ step) * part, part)
        weights = scale_ref[pl.ds(first, part), :]
        for window in range(windows):
            cosine = phase_ref[0, window : window + 1, :]
            sine = phase_ref[1, window : window + 1, :]
            real = rows_ref[window, pl.ds(2 * first, part, stride=2), :]
            imag = rows_ref[window, pl.ds(2 * first + 1, part, stride=2), :]
            weight = weights[:, window : window + 1]
            pieces[step][window, 0] = (weight * (real * cosine + imag * sine)).astype(jnp.bfloat16)
            pieces[step][window, 1] = (weight * (imag * cosine - real * sine)).astype(jnp.bfloat16)


def gather(pieces, held, before):
    windows = pieces[0].shape[0]
    level = lax.rem(lax.axis_index("tm"), TEAM) // SIDES
    for index, piece in enumerate(pieces):
        block = (level ^ (index % LEVELS)) + (before if index < LEVELS else 0)
        held[pl.ds(block * windows, windows)] = piece[...]


def band_sums(left_real, left_imag, right_real, right_imag, table):
    real = left_real[None] * right_real + left_imag[None] * right_imag
    imag = left_imag[None] * right_real - left_real[None] * right_imag
    count, part, freq = real.shape
    cross = jnp.concatenate([real.reshape(count * part, freq), imag.reshape(count * part, freq)], axis=1)
    lagged = jnp.dot(cross, table, preferred_element_type=jnp.float32)
    return jnp.sum((lagged * lagged).reshape(count, part, table.shape[1]), axis=1)


def block_sums(left, left_at, right, right_at, windows, table, store):
    right_real, right_imag = right[pl.ds(right_at, windows), 0], right[pl.ds(right_at, windows), 1]
    for window in range(windows):
        store(window, band_sums(left[left_at + window, 0], left[left_at + window, 1], right_real, right_imag, table))


def level_of(pair, firsts):
    level = jnp.int32(0)
    for first in firsts[1:]:
        level += (pair >= first).astype(jnp.int32)
    start = jnp.int32(0)
    for index, first in enumerate(firsts):
        start = jnp.where(level == index, first, start)
    return level, pair - start


def sweep(counts, unroll, visit):
    firsts = [sum(counts[:index]) for index in range(len(counts))]
    pairs = sum(counts)
    assert pairs % unroll == 0

    def turn(index, carry):
        for inner in range(unroll):
            visit(*level_of(index * unroll + inner, firsts))
        return carry

    lax.fori_loop(0, pairs // unroll, turn, 0)


def near_kernel(teams, count, *refs):
    table_ref, pieces, (sums_ref, held) = refs[0], refs[1 : 1 + count], refs[1 + count :]
    windows = pieces[0].shape[0]
    before = LEVELS if teams else 0
    gather(pieces, held, before)
    table = table_ref[...]
    counts = [LEVELS if teams else level + 1 for level in range(LEVELS)]
    for level in range(LEVELS):
        skipped = (LEVELS - counts[level]) * windows
        if skipped:
            sums_ref[level, :, :skipped, :] = jnp.zeros((windows, skipped, sums_ref.shape[3]), jnp.float32)

    def visit(level, back):
        place = pl.multiple_of((LEVELS - 1 - back) * windows, windows)

        def store(window, sums):
            sums_ref[level, window, pl.ds(place, windows), :] = sums

        block_sums(held, (before + level) * windows, held, (before + level - back) * windows, windows, table, store)

    sweep(counts, 2, visit)


def far_kernel(teams, count, *refs):
    table_ref, near_ref, pieces = refs[0], refs[1], refs[2 : 2 + 2 * count]
    mine_ref, other_ref, held, across, grid = refs[2 + 2 * count :]
    windows = pieces[0].shape[0]
    side = lax.rem(lax.axis_index("tm"), SIDES)
    core = lax.axis_index("chan")
    before = LEVELS if teams else 0
    margin = LEVELS if teams else 1
    gather(pieces[:count], held, before)
    gather(pieces[count:], across, margin)
    if not teams:
        across[pl.ds(0, windows)] = jnp.zeros((windows,) + across.shape[1:], across.dtype)
    table = table_ref[...]
    band = mine_ref.shape[2]
    keep = mine_ref.shape[1]
    reach = LEVELS - 1
    counts = [reach if teams else min(reach, level + 1) for level in range(LEVELS)]
    for level in range(LEVELS):
        for block in range(reach - counts[level]):
            grid[level, :, (2 * block + 1) * windows : (2 * block + 2) * windows, :] = jnp.zeros(
                (windows, windows, grid.shape[3]), jnp.float32
            )

    def visit(level, back):
        place = pl.multiple_of((2 * (reach - 1 - back) + 1) * windows, windows)

        def store(window, sums):
            grid[level, window, pl.ds(place, windows), :] = sums

        right = (margin + level + side - 1 - back) * windows
        block_sums(held, (before + level) * windows, across, right, windows, table, store)

    sweep(counts, 3, visit)

    def finish(level, carry):
        for block in range(LEVELS):
            grid[level, :, 2 * block * windows : (2 * block + 1) * windows, :] = near_ref[
                level, :, block * windows : (block + 1) * windows, :
            ]
        for inner in range(keep):
            window = core * keep + inner
            mine_ref[level, inner] = grid[level, window, pl.ds(window, band), :]
            window = (1 - core) * keep + inner
            other_ref[level, inner] = grid[level, window, pl.ds(window, band), :].astype(other_ref.dtype)
        return carry

    lax.fori_loop(0, LEVELS, finish, 0)


def merge_kernel(mine_ref, other_ref, *outs):
    level = lax.rem(lax.axis_index("tm"), TEAM) // SIDES
    for step, out in enumerate(outs):
        at = level ^ step
        out[...] = (mine_ref[at] + other_ref[at].astype(jnp.float32)).astype(out.dtype)


def vmem():
    return pl.BlockSpec(memory_space=pltpu.VMEM)


def flip(value, axis, size, bits):
    return lax.ppermute(value, axis, [(source, source ^ bits) for source in range(size)])


def shards(spectra, offsets, channel_group):
    windows, local_chans, _, freq = spectra.shape
    chan_count = lax.axis_size("chan")
    tm_count = lax.axis_size("tm")
    channels = local_chans * chan_count
    part = local_chans // LEVELS
    band = SPAN * windows
    keep = windows // chan_count
    params = pltpu.CompilerParams(vmem_limit_bytes=40 * 1024 * 1024)

    rows = spectra.reshape(windows, 2 * local_chans, freq)
    member = (channel_group[None, :] == jnp.arange(GROUPS, dtype=jnp.int32)[:, None]).astype(jnp.float32)
    power = pl.pallas_call(
        power_kernel,
        out_shape=jax.ShapeDtypeStruct((GROUPS, 128), jnp.float32),
        in_specs=[vmem()] * 2,
        out_specs=vmem(),
        scratch_shapes=[pltpu.VMEM((windows, 2 * local_chans, freq), jnp.float32)],
        compiler_params=params,
        name="power",
    )(rows, member)
    other_power = flip(power, "chan", chan_count, 1)
    piece_shape = jax.ShapeDtypeStruct((windows, 2, part, freq), jnp.bfloat16)
    own = pl.pallas_call(
        functools.partial(align_kernel, GROUPS / (freq * channels)),
        out_shape=[piece_shape] * LEVELS,
        in_specs=[vmem()] * 5,
        out_specs=[vmem()] * LEVELS,
        scratch_shapes=[
            pltpu.VMEM((windows, 2 * local_chans, freq), jnp.float32),
            pltpu.VMEM((local_chans, 128), jnp.float32),
        ],
        compiler_params=params,
        name="align",
    )(rows, member, power, other_power, phases(offsets, freq))

    near = [own[0]] + [None] * (LEVELS - 1)
    far = [None] * LEVELS
    for kind, step in EARLY:
        if kind == "near":
            near[step] = flip(own[step], "tm", tm_count, step * SIDES)
        else:
            far[step] = flip(own[step], "tm", tm_count, step * SIDES + 1)
    for step in LATE:
        far[step] = flip(near[step], "tm", tm_count, 1)
    teams = tm_count > TEAM
    if teams:
        pairs = [(source, source + TEAM) for source in range(tm_count - TEAM)]
        near += [lax.ppermute(piece, "tm", pairs) for piece in near]
        far += [lax.ppermute(piece, "tm", pairs) for piece in far]
    count = len(near)
    held_blocks = count
    across_blocks = count if teams else count + 1
    table = lag_table(freq, LAGS)

    near_sums = pl.pallas_call(
        functools.partial(near_kernel, teams, count),
        out_shape=jax.ShapeDtypeStruct((LEVELS, windows, LEVELS * windows, LAGS), jnp.float32),
        in_specs=[vmem()] * (1 + count),
        out_specs=vmem(),
        scratch_shapes=[
            pltpu.VMEM((held_blocks * windows, 2, part, freq), jnp.bfloat16),
        ],
        compiler_params=params,
        cost_estimate=pl.CostEstimate(flops=2000000000, bytes_accessed=2000000, transcendentals=0),
        name="near",
    )(table, *near)
    sums_shape = (LEVELS, keep, band, LAGS)
    mine, other = pl.pallas_call(
        functools.partial(far_kernel, teams, count),
        out_shape=[
            jax.ShapeDtypeStruct(sums_shape, jnp.float32), jax.ShapeDtypeStruct(sums_shape, jnp.bfloat16)
        ],
        in_specs=[vmem()] * (2 + 2 * count),
        out_specs=[vmem()] * 2,
        scratch_shapes=[
            pltpu.VMEM((held_blocks * windows, 2, part, freq), jnp.bfloat16),
            pltpu.VMEM((across_blocks * windows, 2, part, freq), jnp.bfloat16),
            pltpu.VMEM((LEVELS, windows, (SPAN + 1) * windows, LAGS), jnp.float32),
        ],
        compiler_params=params,
        name="far",
    )(table, near_sums, *near, *far)
    sums = pl.pallas_call(
        merge_kernel,
        out_shape=[
            jax.ShapeDtypeStruct(sums_shape[1:], jnp.float32 if step == 0 else jnp.bfloat16) for step in range(LEVELS)
        ],
        in_specs=[vmem()] * 2,
        out_specs=[vmem()] * LEVELS,
        compiler_params=params,
        name="merge",
    )(mine, flip(other, "chan", chan_count, 1))
    total = sums[0]
    for step in OUT_ORDER:
        total = total + flip(sums[step], "tm", tm_count, step * SIDES).astype(jnp.float32)
    return total * (1.0 / channels)


def solution(mesh):
    placed = (P(("arrays", "tm"), "chan", None, None), P(("arrays", "tm")), P(("arrays", "chan")))
    return jax.shard_map(
        shards,
        mesh=mesh,
        in_specs=placed,
        out_specs=P(("arrays", "tm", "chan"), None, None),
        check_vma=False,
    )
```

```python
import functools
import math

import jax
import jax.numpy as jnp
from jax import lax
from jax.experimental import pallas as pl
from jax.experimental.pallas import tpu as pltpu
from jax.sharding import PartitionSpec as P

LAGS = 128
GROUPS = 8
SPAN = 6
SIDES = 2
LEVELS = 4
TEAM = SIDES * LEVELS
FIRST_LATE = 2
UNROLL = 3
EARLY = (("near", 2), ("far", 0), ("near", 3), ("near", 1), ("far", 1))
LATE = (2, 3)
OUT_ORDER = (2, 3, 1)

epsilon = 1e-05

HIGHEST = lax.Precision.HIGHEST


def lag_table(freq_bins, lag_count):
    frequency = jnp.arange(freq_bins, dtype=jnp.int32)[:, None]
    lag_shift = jnp.arange(lag_count, dtype=jnp.int32)[None, :] - lag_count // 2
    phase_turns = jnp.mod(frequency * lag_shift, 2 * freq_bins).astype(jnp.float32)
    phase_angle = jnp.pi * phase_turns / freq_bins
    normaliser = 1.0 / math.sqrt(freq_bins)
    lag_rows = jnp.concatenate(
        [jnp.cos(phase_angle) * normaliser, -jnp.sin(phase_angle) * normaliser], axis=0
    )
    return lag_rows.astype(jnp.bfloat16)


def phases(offsets, freq_bins):
    frequency = jnp.arange(freq_bins, dtype=jnp.int32)[None, :]
    phase_turns = jnp.mod(offsets[:, None] * frequency, 2 * freq_bins).astype(jnp.float32)
    phase_angle = jnp.pi * phase_turns / freq_bins
    return jnp.stack([jnp.cos(phase_angle), jnp.sin(phase_angle)])


def power_kernel(spectra_ref, member_ref, power_ref, rows_ref):
    windows, rows, _ = spectra_ref.shape
    half = rows // 2
    lane = lax.broadcasted_iota(jnp.int32, power_ref.shape, 1)
    power = jnp.zeros(power_ref.shape, jnp.float32)
    for window in range(windows):
        value = spectra_ref[window].astype(jnp.float32)
        rows_ref[window] = value * value
        squares = rows_ref[window, pl.ds(0, half, stride=2), :] + rows_ref[window, pl.ds(1, half, stride=2), :]
        grouped = jnp.dot(member_ref[...], squares, precision=HIGHEST, preferred_element_type=jnp.float32)
        power = jnp.where(lane == window, jnp.sum(grouped, axis=1, keepdims=True), power)
    power_ref[...] = power


def align_kernel(scale_of_energy, spectra_ref, member_ref, own_ref, other_ref, phase_ref, *rest):
    pieces, (rows_ref, scale_ref) = rest[:LEVELS], rest[LEVELS:]
    windows, rows, _ = spectra_ref.shape
    part = rows // 2 // LEVELS
    level = lax.rem(lax.axis_index("tm"), TEAM) // SIDES
    energy = (own_ref[...] + other_ref[...]) * scale_of_energy
    scale_ref[...] = lax.dot_general(
        member_ref[...], lax.rsqrt(energy + epsilon), (((0,), (0,)), ((), ())),
        precision=HIGHEST, preferred_element_type=jnp.float32,
    )
    for window in range(windows):
        rows_ref[window] = spectra_ref[window].astype(jnp.float32)
    for step in range(LEVELS):
        first = pl.multiple_of((level ^ step) * part, part)
        weights = scale_ref[pl.ds(first, part), :]
        for window in range(windows):
            cosine = phase_ref[0, window : window + 1, :]
            sine = phase_ref[1, window : window + 1, :]
            real = rows_ref[window, pl.ds(2 * first, part, stride=2), :]
            imag = rows_ref[window, pl.ds(2 * first + 1, part, stride=2), :]
            weight = weights[:, window : window + 1]
            pieces[step][window, 0] = (weight * (real * cosine + imag * sine)).astype(jnp.bfloat16)
            pieces[step][window, 1] = (weight * (imag * cosine - real * sine)).astype(jnp.bfloat16)


def gather(pieces, held, before, skip=0):
    windows = pieces[0].shape[0]
    level = lax.rem(lax.axis_index("tm"), TEAM) // SIDES
    for index, piece in enumerate(pieces):
        block = (level ^ ((index + skip) % LEVELS)) + (before if index + skip < LEVELS else 0)
        held[pl.ds(block * windows, windows)] = piece[...]


def band_sums(left_real, left_imag, right_real, right_imag, table):
    real = left_real[None] * right_real + left_imag[None] * right_imag
    imag = left_imag[None] * right_real - left_real[None] * right_imag
    count, part, freq = real.shape
    cross = jnp.concatenate([real.reshape(count * part, freq), imag.reshape(count * part, freq)], axis=1)
    lagged = jnp.dot(cross, table, preferred_element_type=jnp.float32)
    return jnp.sum((lagged * lagged).reshape(count, part, table.shape[1]), axis=1)


def block_sums(left, left_at, right, right_at, windows, table, store):
    right_real, right_imag = right[pl.ds(right_at, windows), 0], right[pl.ds(right_at, windows), 1]
    for window in range(windows):
        store(window, band_sums(left[left_at + window, 0], left[left_at + window, 1], right_real, right_imag, table))


def near_kernel(teams, count, *refs):
    table_ref, pieces, (grid, held) = refs[0], refs[1 : 1 + count], refs[1 + count :]
    windows = pieces[0].shape[0]
    before = LEVELS if teams else 0
    gather(pieces, held, before)
    grid[...] = jnp.zeros(grid.shape, grid.dtype)
    table = table_ref[...]
    furthest = LEVELS - 1

    def block(level, kind):
        return held[pl.ds((before + level) * windows, windows), kind]

    for level in range(LEVELS):
        lefts = (before + level) * windows
        own_real, own_imag = block(level, 0), block(level, 1)
        ring = teams or level == furthest
        for back in range(furthest + 1):
            place = 2 * (furthest - back) * windows
            if 0 < back < furthest and (teams or back <= level):
                right_real, right_imag = block(level - back, 0), block(level - back, 1)
                for window in range(windows):
                    grid[level, window, place : place + windows, :] = band_sums(
                        held[lefts + window, 0], held[lefts + window, 1], right_real, right_imag, table
                    )
        last = 2 * furthest * windows
        if ring:
            old_real, old_imag = block(level - furthest, 0), block(level - furthest, 1)
        for window in range(windows):
            rows = windows if ring else window
            if rows:
                if ring and window:
                    right_real = jnp.concatenate([own_real[:window], old_real[window:]], axis=0)
                    right_imag = jnp.concatenate([own_imag[:window], old_imag[window:]], axis=0)
                elif ring:
                    right_real, right_imag = old_real, old_imag
                else:
                    right_real, right_imag = own_real[:window], own_imag[:window]
                sums = band_sums(held[lefts + window, 0], held[lefts + window, 1], right_real, right_imag, table)
                grid[level, window, last : last + rows, :] = sums
                if ring:
                    grid[level, window, :windows, :] = sums


def list_units(kernel, teams, windows, units_ref):
    member = lax.rem(lax.axis_index("tm"), TEAM)
    side, here = lax.rem(member, SIDES), member // SIDES
    halo = LEVELS if teams else 0
    found = jnp.int32(0)
    reach = LEVELS - 1
    for left in range(LEVELS):
        for back in range(reach):
            right = left - 1 - back + side
            late = (right < 0) | ((lax.rem(right + LEVELS, LEVELS) ^ here) >= FIRST_LATE)
            wanted = (right >= -halo) & (late == (kernel == 1))
            values = (left, (left + halo) * windows, (right + halo) * windows, (2 * (reach - 1 - back) + 1) * windows)
            for index, value in enumerate(values):
                units_ref[4 * found + index] = jnp.int32(value)
            found = jnp.where(wanted, found + 1, found)
    last = jnp.maximum(found - 1, 0)
    for extra in range(UNROLL - 1):
        for index in range(4):
            units_ref[4 * (found + extra) + index] = units_ref[4 * last + index]
    return (found + UNROLL - 1) // UNROLL


def far_kernel(kernel, teams, count, *refs):
    table_ref, _, near, pieces = refs[0], refs[1], refs[2], refs[3 : 3 + count]
    grid, (far, units_ref) = refs[3 + count], refs[-2:]
    windows = grid.shape[1]
    turns = list_units(kernel, teams, windows, units_ref)
    gather(pieces, far, LEVELS if teams else 0, 0 if teams or kernel == 0 else FIRST_LATE)
    table = table_ref[...]

    def turn(index, carry):
        for inner in range(UNROLL):
            at = 4 * (index * UNROLL + inner)
            level = units_ref[at]
            row = pl.multiple_of(units_ref[at + 3], windows)

            def store(window, sums):
                grid[level, window, pl.ds(row, windows), :] = sums

            block_sums(near, units_ref[at + 1], far, units_ref[at + 2], windows, table, store)
        return carry

    lax.fori_loop(0, turns, turn, 0)
    if kernel == 1:
        mine_ref, other_ref = refs[4 + count : 6 + count]
        core = lax.axis_index("chan")
        keep, band = mine_ref.shape[1:3]

        def finish(level, carry):
            for inner in range(keep):
                window = core * keep + inner
                mine_ref[level, inner] = grid[level, window, pl.ds(window, band), :]
                window = (1 - core) * keep + inner
                other_ref[level, inner] = grid[level, window, pl.ds(window, band), :].astype(other_ref.dtype)
            return carry

        lax.fori_loop(0, LEVELS, finish, 0)


def merge_kernel(mine_ref, other_ref, *outs):
    level = lax.rem(lax.axis_index("tm"), TEAM) // SIDES
    for step, out in enumerate(outs):
        at = level ^ step
        out[...] = (mine_ref[at] + other_ref[at].astype(jnp.float32)).astype(out.dtype)


def vmem():
    return pl.BlockSpec(memory_space=pltpu.VMEM)


def flip(value, axis, size, bits):
    return lax.ppermute(value, axis, [(source, source ^ bits) for source in range(size)])


def shards(spectra, offsets, channel_group):
    windows, local_chans, _, freq = spectra.shape
    chan_count = lax.axis_size("chan")
    tm_count = lax.axis_size("tm")
    channels = local_chans * chan_count
    part = local_chans // LEVELS
    band = SPAN * windows
    keep = windows // chan_count
    params = pltpu.CompilerParams(vmem_limit_bytes=40 * 1024 * 1024)

    rows = spectra.reshape(windows, 2 * local_chans, freq)
    member = (channel_group[None, :] == jnp.arange(GROUPS, dtype=jnp.int32)[:, None]).astype(jnp.float32)
    power = pl.pallas_call(
        power_kernel,
        out_shape=jax.ShapeDtypeStruct((GROUPS, 128), jnp.float32),
        in_specs=[vmem()] * 2,
        out_specs=vmem(),
        scratch_shapes=[pltpu.VMEM((windows, 2 * local_chans, freq), jnp.float32)],
        compiler_params=params,
        name="power",
    )(rows, member)
    other_power = flip(power, "chan", chan_count, 1)
    piece_shape = jax.ShapeDtypeStruct((windows, 2, part, freq), jnp.bfloat16)
    own = pl.pallas_call(
        functools.partial(align_kernel, GROUPS / (freq * channels)),
        out_shape=[piece_shape] * LEVELS,
        in_specs=[vmem()] * 5,
        out_specs=[vmem()] * LEVELS,
        scratch_shapes=[
            pltpu.VMEM((windows, 2 * local_chans, freq), jnp.float32),
            pltpu.VMEM((local_chans, 128), jnp.float32),
        ],
        compiler_params=params,
        name="align",
    )(rows, member, power, other_power, phases(offsets, freq))

    near = [own[0]] + [None] * (LEVELS - 1)
    far = [None] * LEVELS
    for kind, step in EARLY:
        if kind == "near":
            near[step] = flip(own[step], "tm", tm_count, step * SIDES)
        else:
            far[step] = flip(own[step], "tm", tm_count, step * SIDES + 1)
    for step in LATE:
        far[step] = flip(near[step], "tm", tm_count, 1)
    teams = tm_count > TEAM
    if teams:
        pairs = [(source, source + TEAM) for source in range(tm_count - TEAM)]
        near += [lax.ppermute(piece, "tm", pairs) for piece in near]
        far += [lax.ppermute(piece, "tm", pairs) for piece in far]
    count = len(near)
    table = lag_table(freq, LAGS)
    held = (count * windows, 2, part, freq)
    grid_shape = jax.ShapeDtypeStruct((LEVELS, windows, (SPAN + 1) * windows, LAGS), jnp.float32)
    sums_shape = (LEVELS, keep, band, LAGS)
    grid, near_held = pl.pallas_call(
        functools.partial(near_kernel, teams, count),
        out_shape=[grid_shape, jax.ShapeDtypeStruct(held, jnp.bfloat16)],
        in_specs=[vmem()] * (1 + count),
        out_specs=[vmem()] * 2,
        compiler_params=params,
        cost_estimate=pl.CostEstimate(flops=2000000000, bytes_accessed=2000000, transcendentals=0),
        name="near",
    )(table, *near)
    for kernel, pieces in enumerate((far[:FIRST_LATE], far if teams else far[FIRST_LATE:])):
        results = [
            jax.ShapeDtypeStruct(sums_shape, jnp.float32), jax.ShapeDtypeStruct(sums_shape, jnp.bfloat16)
        ] * kernel
        grid, *sums = pl.pallas_call(
            functools.partial(far_kernel, kernel, teams, len(pieces)),
            out_shape=[grid_shape] + results,
            in_specs=[vmem()] * (3 + len(pieces)),
            out_specs=[vmem()] * (1 + len(results)),
            scratch_shapes=[
                pltpu.VMEM(held, jnp.bfloat16), pltpu.SMEM((4 * (LEVELS * (LEVELS - 1) + UNROLL),), jnp.int32)
            ],
            input_output_aliases={1: 0},
            compiler_params=params,
            cost_estimate=pl.CostEstimate(flops=1000000000, bytes_accessed=1000000, transcendentals=0),
            name=("far", "late")[kernel],
        )(table, grid, near_held, *pieces)
    mine, other = sums
    sums = pl.pallas_call(
        merge_kernel,
        out_shape=[
            jax.ShapeDtypeStruct(sums_shape[1:], jnp.float32 if step == 0 else jnp.bfloat16) for step in range(LEVELS)
        ],
        in_specs=[vmem()] * 2,
        out_specs=[vmem()] * LEVELS,
        compiler_params=params,
        name="merge",
    )(mine, flip(other, "chan", chan_count, 1))
    total = sums[0]
    for step in OUT_ORDER:
        total = total + flip(sums[step], "tm", tm_count, step * SIDES).astype(jnp.float32)
    return total * (1.0 / channels)


def solution(mesh):
    placed = (P(("arrays", "tm"), "chan", None, None), P(("arrays", "tm")), P(("arrays", "chan")))
    return jax.shard_map(
        shards,
        mesh=mesh,
        in_specs=placed,
        out_specs=P(("arrays", "tm", "chan"), None, None),
        check_vma=False,
    )
```

```python
import functools
import math

import jax
import jax.numpy as jnp
from jax import lax
from jax.experimental import pallas as pl
from jax.experimental.pallas import tpu as pltpu
from jax.sharding import PartitionSpec as P

LAGS = 128
GROUPS = 8
SPAN = 6
SIDES = 2
LEVELS = 4
TEAM = SIDES * LEVELS
FAR_STEPS = ((0, 2), (1, 3))
UNROLL = 3
RAW = (2,)
LATE = 2
UNROLL = 3
EARLY = (("near", 2), ("far", 0), ("near", 3), ("near", 1), ("far", 1))
LATE = (2, 1, 3)
OUT_ORDER = (2, 3, 1)

epsilon = 1e-05

HIGHEST = lax.Precision.HIGHEST


def lag_table(freq_bins, lag_count):
    frequency = jnp.arange(freq_bins, dtype=jnp.int32)[:, None]
    lag_shift = jnp.arange(lag_count, dtype=jnp.int32)[None, :] - lag_count // 2
    phase_turns = jnp.mod(frequency * lag_shift, 2 * freq_bins).astype(jnp.float32)
    phase_angle = jnp.pi * phase_turns / freq_bins
    normaliser = 1.0 / math.sqrt(freq_bins)
    lag_rows = jnp.concatenate(
        [jnp.cos(phase_angle) * normaliser, -jnp.sin(phase_angle) * normaliser], axis=0
    )
    return lag_rows.astype(jnp.bfloat16)


def phases(offsets, freq_bins):
    frequency = jnp.arange(freq_bins, dtype=jnp.int32)[None, :]
    phase_turns = jnp.mod(offsets[:, None] * frequency, 2 * freq_bins).astype(jnp.float32)
    phase_angle = jnp.pi * phase_turns / freq_bins
    return jnp.stack([jnp.cos(phase_angle), jnp.sin(phase_angle)])


def power_kernel(spectra_ref, member_ref, *rest):
    power_ref, rows_ref = rest[-2:]
    windows, rows, _ = spectra_ref.shape
    half = rows // 2
    lane = lax.broadcasted_iota(jnp.int32, power_ref.shape, 1)
    power = jnp.zeros(power_ref.shape, jnp.float32)
    for window in range(windows):
        value = spectra_ref[window].astype(jnp.float32)
        rows_ref[window] = value * value
        squares = rows_ref[window, pl.ds(0, half, stride=2), :] + rows_ref[window, pl.ds(1, half, stride=2), :]
        grouped = jnp.dot(member_ref[...], squares, precision=HIGHEST, preferred_element_type=jnp.float32)
        power = jnp.where(lane == window, jnp.sum(grouped, axis=1, keepdims=True), power)
    power_ref[...] = power


def split_kernel(spectra_ref, *rest):
    pieces, rows_ref = rest[:-1], rest[-1]
    windows, part = pieces[0].shape[0], pieces[0].shape[2]
    level = lax.rem(lax.axis_index("tm"), TEAM) // SIDES
    for index, (step, piece) in enumerate(zip(RAW, pieces)):
        first = pl.multiple_of((level ^ step) * 2 * part, 2 * part)
        for window in range(windows):
            rows_ref[index, window] = spectra_ref[window, pl.ds(first, 2 * part), :].astype(jnp.float32)
            for kind in range(2):
                piece[window, kind] = rows_ref[index, window, pl.ds(kind, part, stride=2), :].astype(jnp.bfloat16)


def rotate(real, imag, weight, cosine, sine):
    return (
        (weight * (real * cosine + imag * sine)).astype(jnp.bfloat16),
        (weight * (imag * cosine - real * sine)).astype(jnp.bfloat16),
    )


def spread(member, scales):
    return lax.dot_general(
        member, scales, (((0,), (0,)), ((), ())), precision=HIGHEST, preferred_element_type=jnp.float32
    )


def align_kernel(scale_of_energy, steps, spectra_ref, member_ref, own_ref, other_ref, phase_ref, offset_ref, *rest):
    pieces, (facts_ref, rows_ref, scale_ref) = rest[-3 - len(steps) : -3], rest[-3:]
    windows, rows, _ = spectra_ref.shape
    part = rows // 2 // LEVELS
    level = lax.rem(lax.axis_index("tm"), TEAM) // SIDES
    energy = (own_ref[...] + other_ref[...]) * scale_of_energy
    scales = lax.rsqrt(energy + epsilon)
    lane = lax.broadcasted_iota(jnp.int32, scales.shape, 1)
    facts_ref[...] = jnp.where(lane < windows, scales, offset_ref[...])
    scale_ref[...] = spread(member_ref[...], scales)
    for window in range(windows):
        rows_ref[window] = spectra_ref[window].astype(jnp.float32)
    for step, piece in zip(steps, pieces):
        first = pl.multiple_of((level ^ step) * part, part)
        weights = scale_ref[pl.ds(first, part), :]
        for window in range(windows):
            piece[window, 0], piece[window, 1] = rotate(
                rows_ref[window, pl.ds(2 * first, part, stride=2), :],
                rows_ref[window, pl.ds(2 * first + 1, part, stride=2), :],
                weights[:, window : window + 1],
                phase_ref[0, window : window + 1, :],
                phase_ref[1, window : window + 1, :],
            )


def align_raw_kernel(raw_ref, member_ref, facts_ref, phase_ref, piece_ref, scale_ref):
    windows, _, part, _ = raw_ref.shape
    level = lax.rem(lax.axis_index("tm"), TEAM) // SIDES
    scale_ref[...] = spread(member_ref[...], facts_ref[...])
    weights = scale_ref[pl.ds(pl.multiple_of(level * part, part), part), :]
    for window in range(windows):
        piece_ref[window, 0], piece_ref[window, 1] = rotate(
            raw_ref[window, 0].astype(jnp.float32),
            raw_ref[window, 1].astype(jnp.float32),
            weights[:, window : window + 1],
            phase_ref[0, window : window + 1, :],
            phase_ref[1, window : window + 1, :],
        )


def gather(pieces, held, before, steps=tuple(range(LEVELS))):
    windows = pieces[0].shape[0]
    level = lax.rem(lax.axis_index("tm"), TEAM) // SIDES
    for index, piece in enumerate(pieces):
        block = (level ^ steps[index % len(steps)]) + (before if index < len(steps) else 0)
        held[pl.ds(block * windows, windows)] = piece[...]


def band_sums(left_real, left_imag, right_real, right_imag, table):
    real = left_real[None] * right_real + left_imag[None] * right_imag
    imag = left_imag[None] * right_real - left_real[None] * right_imag
    count, part, freq = real.shape
    cross = jnp.concatenate([real.reshape(count * part, freq), imag.reshape(count * part, freq)], axis=1)
    lagged = jnp.dot(cross, table, preferred_element_type=jnp.float32)
    return jnp.sum((lagged * lagged).reshape(count, part, table.shape[1]), axis=1)


def block_sums(left, left_at, right, right_at, windows, table, store):
    right_real, right_imag = right[pl.ds(right_at, windows), 0], right[pl.ds(right_at, windows), 1]
    for window in range(windows):
        store(window, band_sums(left[left_at + window, 0], left[left_at + window, 1], right_real, right_imag, table))


def near_kernel(teams, count, *refs):
    table_ref, pieces, (grid, held) = refs[0], refs[1 : 1 + count], refs[1 + count :]
    windows = pieces[0].shape[0]
    before = LEVELS if teams else 0
    gather(pieces, held, before)
    grid[...] = jnp.zeros(grid.shape, grid.dtype)
    table = table_ref[...]
    furthest = LEVELS - 1

    def block(level, kind):
        return held[pl.ds((before + level) * windows, windows), kind]

    for level in range(LEVELS):
        lefts = (before + level) * windows
        own_real, own_imag = block(level, 0), block(level, 1)
        ring = teams or level == furthest
        for back in range(furthest + 1):
            place = 2 * (furthest - back) * windows
            if 0 < back < furthest and (teams or back <= level):
                right_real, right_imag = block(level - back, 0), block(level - back, 1)
                for window in range(windows):
                    grid[level, window, place : place + windows, :] = band_sums(
                        held[lefts + window, 0], held[lefts + window, 1], right_real, right_imag, table
                    )
        last = 2 * furthest * windows
        if ring:
            old_real, old_imag = block(level - furthest, 0), block(level - furthest, 1)
        for window in range(windows):
            rows = windows if ring else window
            if rows:
                if ring and window:
                    right_real = jnp.concatenate([own_real[:window], old_real[window:]], axis=0)
                    right_imag = jnp.concatenate([own_imag[:window], old_imag[window:]], axis=0)
                elif ring:
                    right_real, right_imag = old_real, old_imag
                else:
                    right_real, right_imag = own_real[:window], own_imag[:window]
                sums = band_sums(held[lefts + window, 0], held[lefts + window, 1], right_real, right_imag, table)
                grid[level, window, last : last + rows, :] = sums
                if ring:
                    grid[level, window, :windows, :] = sums


def list_units(kernel, teams, windows, units_ref):
    member = lax.rem(lax.axis_index("tm"), TEAM)
    side, here = lax.rem(member, SIDES), member // SIDES
    halo = LEVELS if teams else 0
    found = jnp.int32(0)
    reach = LEVELS - 1
    for left in range(LEVELS):
        for back in range(reach):
            right = left - 1 - back + side
            late = (right < 0) | (((lax.rem(right + LEVELS, LEVELS) ^ here) & 1) == 1)
            wanted = (right >= -halo) & (late == (kernel == 1))
            values = (left, (left + halo) * windows, (right + halo) * windows, (2 * (reach - 1 - back) + 1) * windows)
            for index, value in enumerate(values):
                units_ref[4 * found + index] = jnp.int32(value)
            found = jnp.where(wanted, found + 1, found)
    last = jnp.maximum(found - 1, 0)
    for extra in range(UNROLL - 1):
        for index in range(4):
            units_ref[4 * (found + extra) + index] = units_ref[4 * last + index]
    return (found + UNROLL - 1) // UNROLL


def far_kernel(kernel, teams, count, *refs):
    table_ref, _, near, pieces = refs[0], refs[1], refs[2], refs[3 : 3 + count]
    grid, (far, units_ref) = refs[3 + count], refs[-2:]
    windows = grid.shape[1]
    turns = list_units(kernel, teams, windows, units_ref)
    if teams and kernel == 1:
        gather(pieces, far, LEVELS)
    else:
        gather(pieces, far, LEVELS if teams else 0, FAR_STEPS[kernel])
    table = table_ref[...]

    def turn(index, carry):
        for inner in range(UNROLL):
            at = 4 * (index * UNROLL + inner)
            level = units_ref[at]
            row = pl.multiple_of(units_ref[at + 3], windows)

            def store(window, sums):
                grid[level, window, pl.ds(row, windows), :] = sums

            block_sums(near, units_ref[at + 1], far, units_ref[at + 2], windows, table, store)
        return carry

    lax.fori_loop(0, turns, turn, 0)
    if kernel == 1:
        mine_ref, other_ref = refs[4 + count : 6 + count]
        core = lax.axis_index("chan")
        keep, band = mine_ref.shape[1:3]

        def finish(level, carry):
            for inner in range(keep):
                window = core * keep + inner
                mine_ref[level, inner] = grid[level, window, pl.ds(window, band), :]
                window = (1 - core) * keep + inner
                other_ref[level, inner] = grid[level, window, pl.ds(window, band), :].astype(other_ref.dtype)
            return carry

        lax.fori_loop(0, LEVELS, finish, 0)


def merge_kernel(mine_ref, other_ref, *outs):
    level = lax.rem(lax.axis_index("tm"), TEAM) // SIDES
    for step, out in enumerate(outs):
        at = level ^ step
        out[...] = (mine_ref[at] + other_ref[at].astype(jnp.float32)).astype(out.dtype)


def vmem():
    return pl.BlockSpec(memory_space=pltpu.VMEM)


def flip(value, axis, size, bits):
    return lax.ppermute(value, axis, [(source, source ^ bits) for source in range(size)])


def shards(spectra, offsets, channel_group):
    windows, local_chans, _, freq = spectra.shape
    chan_count = lax.axis_size("chan")
    tm_count = lax.axis_size("tm")
    channels = local_chans * chan_count
    part = local_chans // LEVELS
    band = SPAN * windows
    keep = windows // chan_count
    params = pltpu.CompilerParams(vmem_limit_bytes=40 * 1024 * 1024)

    rows = spectra.reshape(windows, 2 * local_chans, freq)
    piece_shape = jax.ShapeDtypeStruct((windows, 2, part, freq), jnp.bfloat16)
    raw_own = pl.pallas_call(
        split_kernel,
        out_shape=[piece_shape] * len(RAW),
        in_specs=[vmem()],
        out_specs=[vmem()] * len(RAW),
        scratch_shapes=[pltpu.VMEM((len(RAW), windows, 2 * part, freq), jnp.float32)],
        compiler_params=params,
        name="split",
    )(rows)
    raw = [flip(piece, "tm", tm_count, step * SIDES) for step, piece in zip(RAW, raw_own)]
    member = (channel_group[None, :] == jnp.arange(GROUPS, dtype=jnp.int32)[:, None]).astype(jnp.float32)
    power = pl.pallas_call(
        power_kernel,
        out_shape=jax.ShapeDtypeStruct((GROUPS, 128), jnp.float32),
        in_specs=[vmem()] * (2 + len(RAW)),
        out_specs=vmem(),
        scratch_shapes=[pltpu.VMEM((windows, 2 * local_chans, freq), jnp.float32)],
        compiler_params=params,
        name="power",
    )(rows, member, *raw_own)
    other_power = flip(power, "chan", chan_count, 1)
    lanes = power.shape[1]
    lane = jnp.arange(lanes, dtype=jnp.int32)[:, None] - windows
    offset_row = jnp.sum(jnp.where(lane == jnp.arange(windows, dtype=jnp.int32)[None, :], offsets[None, :], 0), axis=1)
    offset_tile = jnp.broadcast_to(offset_row.astype(jnp.float32)[None, :], power.shape)
    turns = phases(offsets, freq)

    def aligned(steps, *after):
        return pl.pallas_call(
            functools.partial(align_kernel, GROUPS / (freq * channels), steps),
            out_shape=[piece_shape] * len(steps) + [jax.ShapeDtypeStruct(power.shape, jnp.float32)],
            in_specs=[vmem()] * (6 + len(after)),
            out_specs=[vmem()] * (len(steps) + 1),
            scratch_shapes=[
                pltpu.VMEM((windows, 2 * local_chans, freq), jnp.float32),
                pltpu.VMEM((local_chans, lanes), jnp.float32),
            ],
            compiler_params=params,
            name="align",
        )(rows, member, power, other_power, turns, offset_tile, *after)

    own = [None] * LEVELS
    own[3], own[1], own[0], facts = aligned((3, 1, 0))

    near = [own[0]] + [None] * (LEVELS - 1)
    far = [None] * LEVELS
    near[3] = flip(own[3], "tm", tm_count, 3 * SIDES)
    near[1] = flip(own[1], "tm", tm_count, SIDES)
    far[0] = flip(own[0], "tm", tm_count, 1)
    for step, piece in zip(RAW, raw):
        their = flip(facts, "tm", tm_count, step * SIDES)
        near[step] = pl.pallas_call(
            align_raw_kernel,
            out_shape=piece_shape,
            in_specs=[vmem()] * 4,
            out_specs=vmem(),
            scratch_shapes=[pltpu.VMEM((local_chans, lanes), jnp.float32)],
            compiler_params=params,
            name="align_raw",
        )(piece, member, their, phases(their[0, windows : 2 * windows].astype(jnp.int32), freq))
    for step in LATE:
        far[step] = flip(near[step], "tm", tm_count, 1)
    teams = tm_count > TEAM
    if teams:
        pairs = [(source, source + TEAM) for source in range(tm_count - TEAM)]
        near += [lax.ppermute(piece, "tm", pairs) for piece in near]
        far += [lax.ppermute(piece, "tm", pairs) for piece in far]
    count = len(near)
    table = lag_table(freq, LAGS)
    held = (count * windows, 2, part, freq)
    grid_shape = jax.ShapeDtypeStruct((LEVELS, windows, (SPAN + 1) * windows, LAGS), jnp.float32)
    sums_shape = (LEVELS, keep, band, LAGS)
    grid, near_held = pl.pallas_call(
        functools.partial(near_kernel, teams, count),
        out_shape=[grid_shape, jax.ShapeDtypeStruct(held, jnp.bfloat16)],
        in_specs=[vmem()] * (1 + count),
        out_specs=[vmem()] * 2,
        compiler_params=params,
        cost_estimate=pl.CostEstimate(flops=2000000000, bytes_accessed=2000000, transcendentals=0),
        name="near",
    )(table, *near)
    for kernel, pieces in enumerate(([far[step] for step in FAR_STEPS[0]], far if teams else [far[step] for step in FAR_STEPS[1]])):
        results = [
            jax.ShapeDtypeStruct(sums_shape, jnp.float32), jax.ShapeDtypeStruct(sums_shape, jnp.bfloat16)
        ] * kernel
        grid, *sums = pl.pallas_call(
            functools.partial(far_kernel, kernel, teams, len(pieces)),
            out_shape=[grid_shape] + results,
            in_specs=[vmem()] * (3 + len(pieces)),
            out_specs=[vmem()] * (1 + len(results)),
            scratch_shapes=[
                pltpu.VMEM(held, jnp.bfloat16), pltpu.SMEM((4 * (LEVELS * (LEVELS - 1) + UNROLL),), jnp.int32)
            ],
            input_output_aliases={1: 0},
            compiler_params=params,
            cost_estimate=pl.CostEstimate(flops=1000000000, bytes_accessed=1000000, transcendentals=0),
            name=("far", "late")[kernel],
        )(table, grid, near_held, *pieces)
    mine, other = sums
    sums = pl.pallas_call(
        merge_kernel,
        out_shape=[
            jax.ShapeDtypeStruct(sums_shape[1:], jnp.float32 if step == 0 else jnp.bfloat16) for step in range(LEVELS)
        ],
        in_specs=[vmem()] * 2,
        out_specs=[vmem()] * LEVELS,
        compiler_params=params,
        name="merge",
    )(mine, flip(other, "chan", chan_count, 1))
    total = sums[0]
    for step in OUT_ORDER:
        total = total + flip(sums[step], "tm", tm_count, step * SIDES).astype(jnp.float32)
    return total * (1.0 / channels)


def solution(mesh):
    placed = (P(("arrays", "tm"), "chan", None, None), P(("arrays", "tm")), P(("arrays", "chan")))
    return jax.shard_map(
        shards,
        mesh=mesh,
        in_specs=placed,
        out_specs=P(("arrays", "tm", "chan"), None, None),
        check_vma=False,
    )
```

```python
import functools
import math

import jax
import jax.numpy as jnp
from jax import lax
from jax.experimental import pallas as pl
from jax.experimental.pallas import tpu as pltpu
from jax.sharding import PartitionSpec as P

LAGS = 128
GROUPS = 8
SPAN = 6
SIDES = 2
LEVELS = 4
TEAM = SIDES * LEVELS
FAR_STEPS = ((0, 2), (1, 3))
UNROLL = 2
RAW = (2,)
LATE = 2
UNROLL = 2
EARLY = (("near", 2), ("far", 0), ("near", 3), ("near", 1), ("far", 1))
LATE = (2, 1, 3)
OUT_ORDER = (2, 3, 1)

epsilon = 1e-05

HIGHEST = lax.Precision.HIGHEST


def lag_table(freq_bins, lag_count):
    frequency = jnp.arange(freq_bins, dtype=jnp.int32)[:, None]
    lag_shift = jnp.arange(lag_count, dtype=jnp.int32)[None, :] - lag_count // 2
    phase_turns = jnp.mod(frequency * lag_shift, 2 * freq_bins).astype(jnp.float32)
    phase_angle = jnp.pi * phase_turns / freq_bins
    normaliser = 1.0 / math.sqrt(freq_bins)
    lag_rows = jnp.concatenate(
        [jnp.cos(phase_angle) * normaliser, -jnp.sin(phase_angle) * normaliser], axis=0
    )
    return lag_rows.astype(jnp.bfloat16)


def phases(offsets, freq_bins):
    frequency = jnp.arange(freq_bins, dtype=jnp.int32)[None, :]
    phase_turns = jnp.mod(offsets[:, None] * frequency, 2 * freq_bins).astype(jnp.float32)
    phase_angle = jnp.pi * phase_turns / freq_bins
    return jnp.stack([jnp.cos(phase_angle), jnp.sin(phase_angle)])


def power_kernel(spectra_ref, member_ref, *rest):
    power_ref, rows_ref = rest[-2:]
    windows, rows, _ = spectra_ref.shape
    half = rows // 2
    lane = lax.broadcasted_iota(jnp.int32, power_ref.shape, 1)
    power = jnp.zeros(power_ref.shape, jnp.float32)
    for window in range(windows):
        value = spectra_ref[window].astype(jnp.float32)
        rows_ref[window] = value * value
        squares = rows_ref[window, pl.ds(0, half, stride=2), :] + rows_ref[window, pl.ds(1, half, stride=2), :]
        grouped = jnp.dot(member_ref[...], squares, precision=HIGHEST, preferred_element_type=jnp.float32)
        power = jnp.where(lane == window, jnp.sum(grouped, axis=1, keepdims=True), power)
    power_ref[...] = power


def split_kernel(spectra_ref, *rest):
    pieces, rows_ref = rest[:-1], rest[-1]
    windows, part = pieces[0].shape[0], pieces[0].shape[2]
    level = lax.rem(lax.axis_index("tm"), TEAM) // SIDES
    for index, (step, piece) in enumerate(zip(RAW, pieces)):
        first = pl.multiple_of((level ^ step) * 2 * part, 2 * part)
        for window in range(windows):
            rows_ref[index, window] = spectra_ref[window, pl.ds(first, 2 * part), :].astype(jnp.float32)
            for kind in range(2):
                piece[window, kind] = rows_ref[index, window, pl.ds(kind, part, stride=2), :].astype(jnp.bfloat16)


def rotate(real, imag, weight, cosine, sine):
    return (
        (weight * (real * cosine + imag * sine)).astype(jnp.bfloat16),
        (weight * (imag * cosine - real * sine)).astype(jnp.bfloat16),
    )


def spread(member, scales):
    return lax.dot_general(
        member, scales, (((0,), (0,)), ((), ())), precision=HIGHEST, preferred_element_type=jnp.float32
    )


def align_kernel(scale_of_energy, steps, spectra_ref, member_ref, own_ref, other_ref, phase_ref, offset_ref, *rest):
    pieces, (facts_ref, rows_ref, scale_ref) = rest[-3 - len(steps) : -3], rest[-3:]
    windows, rows, _ = spectra_ref.shape
    part = rows // 2 // LEVELS
    level = lax.rem(lax.axis_index("tm"), TEAM) // SIDES
    energy = (own_ref[...] + other_ref[...]) * scale_of_energy
    scales = lax.rsqrt(energy + epsilon)
    lane = lax.broadcasted_iota(jnp.int32, scales.shape, 1)
    facts_ref[...] = jnp.where(lane < windows, scales, offset_ref[...])
    scale_ref[...] = spread(member_ref[...], scales)
    for window in range(windows):
        rows_ref[window] = spectra_ref[window].astype(jnp.float32)
    for step, piece in zip(steps, pieces):
        first = pl.multiple_of((level ^ step) * part, part)
        weights = scale_ref[pl.ds(first, part), :]
        for window in range(windows):
            piece[window, 0], piece[window, 1] = rotate(
                rows_ref[window, pl.ds(2 * first, part, stride=2), :],
                rows_ref[window, pl.ds(2 * first + 1, part, stride=2), :],
                weights[:, window : window + 1],
                phase_ref[0, window : window + 1, :],
                phase_ref[1, window : window + 1, :],
            )


def align_raw_kernel(raw_ref, member_ref, facts_ref, phase_ref, piece_ref, scale_ref):
    windows, _, part, _ = raw_ref.shape
    level = lax.rem(lax.axis_index("tm"), TEAM) // SIDES
    scale_ref[...] = spread(member_ref[...], facts_ref[...])
    weights = scale_ref[pl.ds(pl.multiple_of(level * part, part), part), :]
    for window in range(windows):
        piece_ref[window, 0], piece_ref[window, 1] = rotate(
            raw_ref[window, 0].astype(jnp.float32),
            raw_ref[window, 1].astype(jnp.float32),
            weights[:, window : window + 1],
            phase_ref[0, window : window + 1, :],
            phase_ref[1, window : window + 1, :],
        )


def gather(pieces, held, before, steps=tuple(range(LEVELS))):
    windows = pieces[0].shape[0]
    level = lax.rem(lax.axis_index("tm"), TEAM) // SIDES
    for index, piece in enumerate(pieces):
        block = (level ^ steps[index % len(steps)]) + (before if index < len(steps) else 0)
        held[pl.ds(block * windows, windows)] = piece[...]


def band_sums(left_real, left_imag, right_real, right_imag, table):
    real = left_real[None] * right_real + left_imag[None] * right_imag
    imag = left_imag[None] * right_real - left_real[None] * right_imag
    count, part, freq = real.shape
    cross = jnp.concatenate([real.reshape(count * part, freq), imag.reshape(count * part, freq)], axis=1)
    lagged = jnp.dot(cross, table, preferred_element_type=jnp.float32)
    return jnp.sum((lagged * lagged).reshape(count, part, table.shape[1]), axis=1)


def block_sums(left, left_at, right, right_at, windows, table, store):
    right_real, right_imag = right[pl.ds(right_at, windows), 0], right[pl.ds(right_at, windows), 1]
    for window in range(windows):
        store(window, band_sums(left[left_at + window, 0], left[left_at + window, 1], right_real, right_imag, table))


def near_kernel(teams, count, *refs):
    table_ref, pieces, (grid, held) = refs[0], refs[1 : 1 + count], refs[1 + count :]
    windows = pieces[0].shape[0]
    before = LEVELS if teams else 0
    gather(pieces, held, before)
    grid[...] = jnp.zeros(grid.shape, grid.dtype)
    table = table_ref[...]
    furthest = LEVELS - 1

    def block(level, kind):
        return held[pl.ds((before + level) * windows, windows), kind]

    for level in range(LEVELS):
        lefts = (before + level) * windows
        own_real, own_imag = block(level, 0), block(level, 1)
        ring = teams or level == furthest
        for back in range(furthest + 1):
            place = 2 * (furthest - back) * windows
            if 0 < back < furthest and (teams or back <= level):
                right_real, right_imag = block(level - back, 0), block(level - back, 1)
                for window in range(windows):
                    grid[level, window, place : place + windows, :] = band_sums(
                        held[lefts + window, 0], held[lefts + window, 1], right_real, right_imag, table
                    )
        last = 2 * furthest * windows
        if ring:
            old_real, old_imag = block(level - furthest, 0), block(level - furthest, 1)
        for window in range(windows):
            rows = windows if ring else window
            if rows:
                if ring and window:
                    right_real = jnp.concatenate([own_real[:window], old_real[window:]], axis=0)
                    right_imag = jnp.concatenate([own_imag[:window], old_imag[window:]], axis=0)
                elif ring:
                    right_real, right_imag = old_real, old_imag
                else:
                    right_real, right_imag = own_real[:window], own_imag[:window]
                sums = band_sums(held[lefts + window, 0], held[lefts + window, 1], right_real, right_imag, table)
                grid[level, window, last : last + rows, :] = sums
                if ring:
                    grid[level, window, :windows, :] = sums


def list_units(kernel, teams, windows, units_ref):
    member = lax.rem(lax.axis_index("tm"), TEAM)
    side, here = lax.rem(member, SIDES), member // SIDES
    halo = LEVELS if teams else 0
    found = jnp.int32(0)
    reach = LEVELS - 1
    for left in range(LEVELS):
        for back in range(reach):
            right = left - 1 - back + side
            late = (right < 0) | (((lax.rem(right + LEVELS, LEVELS) ^ here) & 1) == 1)
            wanted = (right >= -halo) & (late == (kernel == 1))
            values = (left, (left + halo) * windows, (right + halo) * windows, (2 * (reach - 1 - back) + 1) * windows)
            for index, value in enumerate(values):
                units_ref[4 * found + index] = jnp.int32(value)
            found = jnp.where(wanted, found + 1, found)
    last = jnp.maximum(found - 1, 0)
    for extra in range(UNROLL - 1):
        for index in range(4):
            units_ref[4 * (found + extra) + index] = units_ref[4 * last + index]
    return (found + UNROLL - 1) // UNROLL


def far_kernel(kernel, teams, count, *refs):
    table_ref, _, near, pieces = refs[0], refs[1], refs[2], refs[3 : 3 + count]
    grid, (far, units_ref) = refs[3 + count], refs[-2:]
    windows = grid.shape[1]
    turns = list_units(kernel, teams, windows, units_ref)
    if teams and kernel == 1:
        gather(pieces, far, LEVELS)
    else:
        gather(pieces, far, LEVELS if teams else 0, FAR_STEPS[kernel])
    table = table_ref[...]

    def turn(index, carry):
        for inner in range(UNROLL):
            at = 4 * (index * UNROLL + inner)
            level = units_ref[at]
            row = pl.multiple_of(units_ref[at + 3], windows)

            def store(window, sums):
                grid[level, window, pl.ds(row, windows), :] = sums

            block_sums(near, units_ref[at + 1], far, units_ref[at + 2], windows, table, store)
        return carry

    lax.fori_loop(0, turns, turn, 0)
    if kernel == 1:
        mine_ref, other_ref = refs[4 + count : 6 + count]
        core = lax.axis_index("chan")
        keep, band = mine_ref.shape[1:3]

        def finish(level, carry):
            for inner in range(keep):
                window = core * keep + inner
                mine_ref[level, inner] = grid[level, window, pl.ds(window, band), :]
                window = (1 - core) * keep + inner
                other_ref[level, inner] = grid[level, window, pl.ds(window, band), :].astype(other_ref.dtype)
            return carry

        lax.fori_loop(0, LEVELS, finish, 0)


def merge_kernel(mine_ref, other_ref, *outs):
    level = lax.rem(lax.axis_index("tm"), TEAM) // SIDES
    for step, out in enumerate(outs):
        at = level ^ step
        out[...] = (mine_ref[at] + other_ref[at].astype(jnp.float32)).astype(out.dtype)


def vmem():
    return pl.BlockSpec(memory_space=pltpu.VMEM)


def flip(value, axis, size, bits):
    return lax.ppermute(value, axis, [(source, source ^ bits) for source in range(size)])


def shards(spectra, offsets, channel_group):
    windows, local_chans, _, freq = spectra.shape
    chan_count = lax.axis_size("chan")
    tm_count = lax.axis_size("tm")
    channels = local_chans * chan_count
    part = local_chans // LEVELS
    band = SPAN * windows
    keep = windows // chan_count
    params = pltpu.CompilerParams(vmem_limit_bytes=40 * 1024 * 1024)

    rows = spectra.reshape(windows, 2 * local_chans, freq)
    piece_shape = jax.ShapeDtypeStruct((windows, 2, part, freq), jnp.bfloat16)
    raw_own = pl.pallas_call(
        split_kernel,
        out_shape=[piece_shape] * len(RAW),
        in_specs=[vmem()],
        out_specs=[vmem()] * len(RAW),
        scratch_shapes=[pltpu.VMEM((len(RAW), windows, 2 * part, freq), jnp.float32)],
        compiler_params=params,
        name="split",
    )(rows)
    raw = [flip(piece, "tm", tm_count, step * SIDES) for step, piece in zip(RAW, raw_own)]
    member = (channel_group[None, :] == jnp.arange(GROUPS, dtype=jnp.int32)[:, None]).astype(jnp.float32)
    power = pl.pallas_call(
        power_kernel,
        out_shape=jax.ShapeDtypeStruct((GROUPS, 128), jnp.float32),
        in_specs=[vmem()] * (2 + len(RAW)),
        out_specs=vmem(),
        scratch_shapes=[pltpu.VMEM((windows, 2 * local_chans, freq), jnp.float32)],
        compiler_params=params,
        name="power",
    )(rows, member, *raw_own)
    other_power = flip(power, "chan", chan_count, 1)
    lanes = power.shape[1]
    lane = jnp.arange(lanes, dtype=jnp.int32)[:, None] - windows
    offset_row = jnp.sum(jnp.where(lane == jnp.arange(windows, dtype=jnp.int32)[None, :], offsets[None, :], 0), axis=1)
    offset_tile = jnp.broadcast_to(offset_row.astype(jnp.float32)[None, :], power.shape)
    turns = phases(offsets, freq)

    def aligned(steps, *after):
        return pl.pallas_call(
            functools.partial(align_kernel, GROUPS / (freq * channels), steps),
            out_shape=[piece_shape] * len(steps) + [jax.ShapeDtypeStruct(power.shape, jnp.float32)],
            in_specs=[vmem()] * (6 + len(after)),
            out_specs=[vmem()] * (len(steps) + 1),
            scratch_shapes=[
                pltpu.VMEM((windows, 2 * local_chans, freq), jnp.float32),
                pltpu.VMEM((local_chans, lanes), jnp.float32),
            ],
            compiler_params=params,
            name="align",
        )(rows, member, power, other_power, turns, offset_tile, *after)

    own = [None] * LEVELS
    own[3], own[1], own[0], facts = aligned((3, 1, 0))

    near = [own[0]] + [None] * (LEVELS - 1)
    far = [None] * LEVELS
    near[3] = flip(own[3], "tm", tm_count, 3 * SIDES)
    near[1] = flip(own[1], "tm", tm_count, SIDES)
    far[0] = flip(own[0], "tm", tm_count, 1)
    for step, piece in zip(RAW, raw):
        their = flip(facts, "tm", tm_count, step * SIDES)
        near[step] = pl.pallas_call(
            align_raw_kernel,
            out_shape=piece_shape,
            in_specs=[vmem()] * 4,
            out_specs=vmem(),
            scratch_shapes=[pltpu.VMEM((local_chans, lanes), jnp.float32)],
            compiler_params=params,
            name="align_raw",
        )(piece, member, their, phases(their[0, windows : 2 * windows].astype(jnp.int32), freq))
    for step in LATE:
        far[step] = flip(near[step], "tm", tm_count, 1)
    teams = tm_count > TEAM
    if teams:
        pairs = [(source, source + TEAM) for source in range(tm_count - TEAM)]
        near += [lax.ppermute(piece, "tm", pairs) for piece in near]
        far += [lax.ppermute(piece, "tm", pairs) for piece in far]
    count = len(near)
    table = lag_table(freq, LAGS)
    held = (count * windows, 2, part, freq)
    grid_shape = jax.ShapeDtypeStruct((LEVELS, windows, (SPAN + 1) * windows, LAGS), jnp.float32)
    sums_shape = (LEVELS, keep, band, LAGS)
    grid, near_held = pl.pallas_call(
        functools.partial(near_kernel, teams, count),
        out_shape=[grid_shape, jax.ShapeDtypeStruct(held, jnp.bfloat16)],
        in_specs=[vmem()] * (1 + count),
        out_specs=[vmem()] * 2,
        compiler_params=params,
        cost_estimate=pl.CostEstimate(flops=2000000000, bytes_accessed=2000000, transcendentals=0),
        name="near",
    )(table, *near)
    for kernel, pieces in enumerate(([far[step] for step in FAR_STEPS[0]], far if teams else [far[step] for step in FAR_STEPS[1]])):
        results = [
            jax.ShapeDtypeStruct(sums_shape, jnp.float32), jax.ShapeDtypeStruct(sums_shape, jnp.bfloat16)
        ] * kernel
        grid, *sums = pl.pallas_call(
            functools.partial(far_kernel, kernel, teams, len(pieces)),
            out_shape=[grid_shape] + results,
            in_specs=[vmem()] * (3 + len(pieces)),
            out_specs=[vmem()] * (1 + len(results)),
            scratch_shapes=[
                pltpu.VMEM(held, jnp.bfloat16), pltpu.SMEM((4 * (LEVELS * (LEVELS - 1) + UNROLL),), jnp.int32)
            ],
            input_output_aliases={1: 0},
            compiler_params=params,
            cost_estimate=pl.CostEstimate(flops=1000000000, bytes_accessed=1000000, transcendentals=0),
            name=("far", "late")[kernel],
        )(table, grid, near_held, *pieces)
    mine, other = sums
    sums = pl.pallas_call(
        merge_kernel,
        out_shape=[
            jax.ShapeDtypeStruct(sums_shape[1:], jnp.float32 if step == 0 else jnp.bfloat16) for step in range(LEVELS)
        ],
        in_specs=[vmem()] * 2,
        out_specs=[vmem()] * LEVELS,
        compiler_params=params,
        name="merge",
    )(mine, flip(other, "chan", chan_count, 1))
    total = sums[0]
    for step in OUT_ORDER:
        total = total + flip(sums[step], "tm", tm_count, step * SIDES).astype(jnp.float32)
    return total * (1.0 / channels)


def solution(mesh):
    placed = (P(("arrays", "tm"), "chan", None, None), P(("arrays", "tm")), P(("arrays", "chan")))
    return jax.shard_map(
        shards,
        mesh=mesh,
        in_specs=placed,
        out_specs=P(("arrays", "tm", "chan"), None, None),
        check_vma=False,
    )
```

```python
import functools
import math

import jax
import jax.numpy as jnp
from jax import lax
from jax.experimental import pallas as pl
from jax.experimental.pallas import tpu as pltpu
from jax.sharding import PartitionSpec as P

LAGS = 128
GROUPS = 8
SPAN = 6
SIDES = 2
LEVELS = 4
TEAM = SIDES * LEVELS
FAR_STEPS = ((0, 2), (1, 3))
UNROLL = 2
RAW = (2,)
LATE = 2
UNROLL = 2
EARLY = (("near", 2), ("far", 0), ("near", 3), ("near", 1), ("far", 1))
LATE = (2, 1, 3)
OUT_ORDER = (2, 3, 1)

epsilon = 1e-05

HIGHEST = lax.Precision.HIGHEST


def lag_table(freq_bins, lag_count):
    frequency = jnp.arange(freq_bins, dtype=jnp.int32)[:, None]
    lag_shift = jnp.arange(lag_count, dtype=jnp.int32)[None, :] - lag_count // 2
    phase_turns = jnp.mod(frequency * lag_shift, 2 * freq_bins).astype(jnp.float32)
    phase_angle = jnp.pi * phase_turns / freq_bins
    normaliser = 1.0 / math.sqrt(freq_bins)
    lag_rows = jnp.concatenate(
        [jnp.cos(phase_angle) * normaliser, -jnp.sin(phase_angle) * normaliser], axis=0
    )
    return lag_rows.astype(jnp.bfloat16)


def phases(offsets, freq_bins):
    frequency = jnp.arange(freq_bins, dtype=jnp.int32)[None, :]
    phase_turns = jnp.mod(offsets[:, None] * frequency, 2 * freq_bins).astype(jnp.float32)
    phase_angle = jnp.pi * phase_turns / freq_bins
    return jnp.stack([jnp.cos(phase_angle), jnp.sin(phase_angle)])


def power_kernel(spectra_ref, member_ref, *rest):
    power_ref, rows_ref = rest[-2:]
    windows, rows, _ = spectra_ref.shape
    half = rows // 2
    lane = lax.broadcasted_iota(jnp.int32, power_ref.shape, 1)
    power = jnp.zeros(power_ref.shape, jnp.float32)
    for window in range(windows):
        value = spectra_ref[window].astype(jnp.float32)
        rows_ref[window] = value * value
        squares = rows_ref[window, pl.ds(0, half, stride=2), :] + rows_ref[window, pl.ds(1, half, stride=2), :]
        grouped = jnp.dot(member_ref[...], squares, precision=HIGHEST, preferred_element_type=jnp.float32)
        power = jnp.where(lane == window, jnp.sum(grouped, axis=1, keepdims=True), power)
    power_ref[...] = power


def split_kernel(spectra_ref, *rest):
    pieces, rows_ref = rest[:-1], rest[-1]
    windows, part = pieces[0].shape[0], pieces[0].shape[2]
    level = lax.rem(lax.axis_index("tm"), TEAM) // SIDES
    for index, (step, piece) in enumerate(zip(RAW, pieces)):
        first = pl.multiple_of((level ^ step) * 2 * part, 2 * part)
        for window in range(windows):
            rows_ref[index, window] = spectra_ref[window, pl.ds(first, 2 * part), :].astype(jnp.float32)
            for kind in range(2):
                piece[window, kind] = rows_ref[index, window, pl.ds(kind, part, stride=2), :].astype(jnp.bfloat16)


def rotate(real, imag, weight, cosine, sine):
    return (
        (weight * (real * cosine + imag * sine)).astype(jnp.bfloat16),
        (weight * (imag * cosine - real * sine)).astype(jnp.bfloat16),
    )


def spread(member, scales):
    return lax.dot_general(
        member, scales, (((0,), (0,)), ((), ())), precision=HIGHEST, preferred_element_type=jnp.float32
    )


def align_kernel(scale_of_energy, steps, spectra_ref, member_ref, own_ref, other_ref, phase_ref, offset_ref, *rest):
    pieces, (facts_ref, rows_ref, scale_ref) = rest[-3 - len(steps) : -3], rest[-3:]
    windows, rows, _ = spectra_ref.shape
    part = rows // 2 // LEVELS
    level = lax.rem(lax.axis_index("tm"), TEAM) // SIDES
    energy = (own_ref[...] + other_ref[...]) * scale_of_energy
    scales = lax.rsqrt(energy + epsilon)
    lane = lax.broadcasted_iota(jnp.int32, scales.shape, 1)
    facts_ref[...] = jnp.where(lane < windows, scales, offset_ref[...])
    scale_ref[...] = spread(member_ref[...], scales)
    for window in range(windows):
        rows_ref[window] = spectra_ref[window].astype(jnp.float32)
    for step, piece in zip(steps, pieces):
        first = pl.multiple_of((level ^ step) * part, part)
        weights = scale_ref[pl.ds(first, part), :]
        for window in range(windows):
            piece[window, 0], piece[window, 1] = rotate(
                rows_ref[window, pl.ds(2 * first, part, stride=2), :],
                rows_ref[window, pl.ds(2 * first + 1, part, stride=2), :],
                weights[:, window : window + 1],
                phase_ref[0, window : window + 1, :],
                phase_ref[1, window : window + 1, :],
            )


def align_raw_kernel(raw_ref, member_ref, facts_ref, phase_ref, piece_ref, scale_ref):
    windows, _, part, _ = raw_ref.shape
    level = lax.rem(lax.axis_index("tm"), TEAM) // SIDES
    scale_ref[...] = spread(member_ref[...], facts_ref[...])
    weights = scale_ref[pl.ds(pl.multiple_of(level * part, part), part), :]
    for window in range(windows):
        piece_ref[window, 0], piece_ref[window, 1] = rotate(
            raw_ref[window, 0].astype(jnp.float32),
            raw_ref[window, 1].astype(jnp.float32),
            weights[:, window : window + 1],
            phase_ref[0, window : window + 1, :],
            phase_ref[1, window : window + 1, :],
        )


def gather(pieces, held, before, steps=tuple(range(LEVELS))):
    windows = pieces[0].shape[0]
    level = lax.rem(lax.axis_index("tm"), TEAM) // SIDES
    for index, piece in enumerate(pieces):
        block = (level ^ steps[index % len(steps)]) + (before if index < len(steps) else 0)
        held[pl.ds(block * windows, windows)] = piece[...]


def band_sums(left_real, left_imag, right_real, right_imag, table):
    real = left_real[None] * right_real + left_imag[None] * right_imag
    imag = left_imag[None] * right_real - left_real[None] * right_imag
    count, part, freq = real.shape
    cross = jnp.concatenate([real.reshape(count * part, freq), imag.reshape(count * part, freq)], axis=1)
    lagged = jnp.dot(cross, table, preferred_element_type=jnp.float32)
    return jnp.sum((lagged * lagged).reshape(count, part, table.shape[1]), axis=1)


def block_sums(left, left_at, right, right_at, windows, table, store):
    right_real, right_imag = right[pl.ds(right_at, windows), 0], right[pl.ds(right_at, windows), 1]
    for window in range(windows):
        store(window, band_sums(left[left_at + window, 0], left[left_at + window, 1], right_real, right_imag, table))


def near_kernel(teams, count, *refs):
    table_ref, pieces, (grid, held) = refs[0], refs[1 : 1 + count], refs[1 + count :]
    windows = pieces[0].shape[0]
    before = LEVELS if teams else 0
    gather(pieces, held, before)
    grid[...] = jnp.zeros(grid.shape, grid.dtype)
    table = table_ref[...]
    furthest = LEVELS - 1

    def block(level, kind):
        return held[pl.ds((before + level) * windows, windows), kind]

    for level in range(LEVELS):
        lefts = (before + level) * windows
        own_real, own_imag = block(level, 0), block(level, 1)
        ring = teams or level == furthest
        for back in range(furthest + 1):
            place = 2 * (furthest - back) * windows
            if 0 < back < furthest and (teams or back <= level):
                right_real, right_imag = block(level - back, 0), block(level - back, 1)
                for window in range(windows):
                    grid[level, window, place : place + windows, :] = band_sums(
                        held[lefts + window, 0], held[lefts + window, 1], right_real, right_imag, table
                    )
        last = 2 * furthest * windows
        if ring:
            old_real, old_imag = block(level - furthest, 0), block(level - furthest, 1)
        for window in range(windows):
            rows = windows if ring else window
            if rows:
                if ring and window:
                    right_real = jnp.concatenate([own_real[:window], old_real[window:]], axis=0)
                    right_imag = jnp.concatenate([own_imag[:window], old_imag[window:]], axis=0)
                elif ring:
                    right_real, right_imag = old_real, old_imag
                else:
                    right_real, right_imag = own_real[:window], own_imag[:window]
                sums = band_sums(held[lefts + window, 0], held[lefts + window, 1], right_real, right_imag, table)
                grid[level, window, last : last + rows, :] = sums
                if ring:
                    grid[level, window, :windows, :] = sums


def list_units(kernel, teams, windows, units_ref):
    member = lax.rem(lax.axis_index("tm"), TEAM)
    side, here = lax.rem(member, SIDES), member // SIDES
    halo = LEVELS if teams else 0
    found = jnp.int32(0)
    reach = LEVELS - 1
    for left in range(LEVELS):
        for back in range(reach):
            right = left - 1 - back + side
            late = (right < 0) | (((lax.rem(right + LEVELS, LEVELS) ^ here) & 1) == 1)
            wanted = (right >= -halo) & (late == (kernel == 1))
            values = (left, (left + halo) * windows, (right + halo) * windows, (2 * (reach - 1 - back) + 1) * windows)
            for index, value in enumerate(values):
                units_ref[4 * found + index] = jnp.int32(value)
            found = jnp.where(wanted, found + 1, found)
    return found


def far_kernel(kernel, teams, count, *refs):
    table_ref, _, near, pieces = refs[0], refs[1], refs[2], refs[3 : 3 + count]
    grid, (far, units_ref) = refs[3 + count], refs[-2:]
    windows = grid.shape[1]
    found = list_units(kernel, teams, windows, units_ref)
    if teams and kernel == 1:
        gather(pieces, far, LEVELS)
    else:
        gather(pieces, far, LEVELS if teams else 0, FAR_STEPS[kernel])
    table = table_ref[...]

    def unit(at):
        level = units_ref[at]
        row = pl.multiple_of(units_ref[at + 3], windows)

        def store(window, sums):
            grid[level, window, pl.ds(row, windows), :] = sums

        block_sums(near, units_ref[at + 1], far, units_ref[at + 2], windows, table, store)

    def turn(index, carry):
        for inner in range(UNROLL):
            unit(4 * (index * UNROLL + inner))
        return carry

    def single(index, carry):
        unit(4 * index)
        return carry

    turns = found // UNROLL
    lax.fori_loop(0, turns, turn, 0)
    lax.fori_loop(turns * UNROLL, found, single, 0)
    if kernel == 1:
        mine_ref, other_ref = refs[4 + count : 6 + count]
        core = lax.axis_index("chan")
        keep, band = mine_ref.shape[1:3]

        def finish(level, carry):
            for inner in range(keep):
                window = core * keep + inner
                mine_ref[level, inner] = grid[level, window, pl.ds(window, band), :]
                window = (1 - core) * keep + inner
                other_ref[level, inner] = grid[level, window, pl.ds(window, band), :].astype(other_ref.dtype)
            return carry

        lax.fori_loop(0, LEVELS, finish, 0)


def merge_kernel(mine_ref, other_ref, *outs):
    level = lax.rem(lax.axis_index("tm"), TEAM) // SIDES
    for step, out in enumerate(outs):
        at = level ^ step
        out[...] = (mine_ref[at] + other_ref[at].astype(jnp.float32)).astype(out.dtype)


def vmem():
    return pl.BlockSpec(memory_space=pltpu.VMEM)


def flip(value, axis, size, bits):
    return lax.ppermute(value, axis, [(source, source ^ bits) for source in range(size)])


def shards(spectra, offsets, channel_group):
    windows, local_chans, _, freq = spectra.shape
    chan_count = lax.axis_size("chan")
    tm_count = lax.axis_size("tm")
    channels = local_chans * chan_count
    part = local_chans // LEVELS
    band = SPAN * windows
    keep = windows // chan_count
    params = pltpu.CompilerParams(vmem_limit_bytes=40 * 1024 * 1024)

    rows = spectra.reshape(windows, 2 * local_chans, freq)
    piece_shape = jax.ShapeDtypeStruct((windows, 2, part, freq), jnp.bfloat16)
    raw_own = pl.pallas_call(
        split_kernel,
        out_shape=[piece_shape] * len(RAW),
        in_specs=[vmem()],
        out_specs=[vmem()] * len(RAW),
        scratch_shapes=[pltpu.VMEM((len(RAW), windows, 2 * part, freq), jnp.float32)],
        compiler_params=params,
        name="split",
    )(rows)
    raw = [flip(piece, "tm", tm_count, step * SIDES) for step, piece in zip(RAW, raw_own)]
    member = (channel_group[None, :] == jnp.arange(GROUPS, dtype=jnp.int32)[:, None]).astype(jnp.float32)
    power = pl.pallas_call(
        power_kernel,
        out_shape=jax.ShapeDtypeStruct((GROUPS, 128), jnp.float32),
        in_specs=[vmem()] * (2 + len(RAW)),
        out_specs=vmem(),
        scratch_shapes=[pltpu.VMEM((windows, 2 * local_chans, freq), jnp.float32)],
        compiler_params=params,
        name="power",
    )(rows, member, *raw_own)
    other_power = flip(power, "chan", chan_count, 1)
    lanes = power.shape[1]
    lane = jnp.arange(lanes, dtype=jnp.int32)[:, None] - windows
    offset_row = jnp.sum(jnp.where(lane == jnp.arange(windows, dtype=jnp.int32)[None, :], offsets[None, :], 0), axis=1)
    offset_tile = jnp.broadcast_to(offset_row.astype(jnp.float32)[None, :], power.shape)
    turns = phases(offsets, freq)

    def aligned(steps, *after):
        return pl.pallas_call(
            functools.partial(align_kernel, GROUPS / (freq * channels), steps),
            out_shape=[piece_shape] * len(steps) + [jax.ShapeDtypeStruct(power.shape, jnp.float32)],
            in_specs=[vmem()] * (6 + len(after)),
            out_specs=[vmem()] * (len(steps) + 1),
            scratch_shapes=[
                pltpu.VMEM((windows, 2 * local_chans, freq), jnp.float32),
                pltpu.VMEM((local_chans, lanes), jnp.float32),
            ],
            compiler_params=params,
            name="align",
        )(rows, member, power, other_power, turns, offset_tile, *after)

    own = [None] * LEVELS
    own[3], own[1], own[0], facts = aligned((3, 1, 0))

    near = [own[0]] + [None] * (LEVELS - 1)
    far = [None] * LEVELS
    near[3] = flip(own[3], "tm", tm_count, 3 * SIDES)
    near[1] = flip(own[1], "tm", tm_count, SIDES)
    far[0] = flip(own[0], "tm", tm_count, 1)
    for step, piece in zip(RAW, raw):
        their = flip(facts, "tm", tm_count, step * SIDES)
        near[step] = pl.pallas_call(
            align_raw_kernel,
            out_shape=piece_shape,
            in_specs=[vmem()] * 4,
            out_specs=vmem(),
            scratch_shapes=[pltpu.VMEM((local_chans, lanes), jnp.float32)],
            compiler_params=params,
            name="align_raw",
        )(piece, member, their, phases(their[0, windows : 2 * windows].astype(jnp.int32), freq))
    for step in LATE:
        far[step] = flip(near[step], "tm", tm_count, 1)
    teams = tm_count > TEAM
    if teams:
        pairs = [(source, source + TEAM) for source in range(tm_count - TEAM)]
        near += [lax.ppermute(piece, "tm", pairs) for piece in near]
        far += [lax.ppermute(piece, "tm", pairs) for piece in far]
    count = len(near)
    table = lag_table(freq, LAGS)
    held = (count * windows, 2, part, freq)
    grid_shape = jax.ShapeDtypeStruct((LEVELS, windows, (SPAN + 1) * windows, LAGS), jnp.float32)
    sums_shape = (LEVELS, keep, band, LAGS)
    grid, near_held = pl.pallas_call(
        functools.partial(near_kernel, teams, count),
        out_shape=[grid_shape, jax.ShapeDtypeStruct(held, jnp.bfloat16)],
        in_specs=[vmem()] * (1 + count),
        out_specs=[vmem()] * 2,
        compiler_params=params,
        cost_estimate=pl.CostEstimate(flops=2000000000, bytes_accessed=2000000, transcendentals=0),
        name="near",
    )(table, *near)
    for kernel, pieces in enumerate(([far[step] for step in FAR_STEPS[0]], far if teams else [far[step] for step in FAR_STEPS[1]])):
        results = [
            jax.ShapeDtypeStruct(sums_shape, jnp.float32), jax.ShapeDtypeStruct(sums_shape, jnp.bfloat16)
        ] * kernel
        grid, *sums = pl.pallas_call(
            functools.partial(far_kernel, kernel, teams, len(pieces)),
            out_shape=[grid_shape] + results,
            in_specs=[vmem()] * (3 + len(pieces)),
            out_specs=[vmem()] * (1 + len(results)),
            scratch_shapes=[
                pltpu.VMEM(held, jnp.bfloat16), pltpu.SMEM((4 * (LEVELS * (LEVELS - 1) + UNROLL),), jnp.int32)
            ],
            input_output_aliases={1: 0},
            compiler_params=params,
            cost_estimate=pl.CostEstimate(flops=1000000000, bytes_accessed=1000000, transcendentals=0),
            name=("far", "late")[kernel],
        )(table, grid, near_held, *pieces)
    mine, other = sums
    sums = pl.pallas_call(
        merge_kernel,
        out_shape=[
            jax.ShapeDtypeStruct(sums_shape[1:], jnp.float32 if step == 0 else jnp.bfloat16) for step in range(LEVELS)
        ],
        in_specs=[vmem()] * 2,
        out_specs=[vmem()] * LEVELS,
        compiler_params=params,
        name="merge",
    )(mine, flip(other, "chan", chan_count, 1))
    total = sums[0]
    for step in OUT_ORDER:
        total = total + flip(sums[step], "tm", tm_count, step * SIDES).astype(jnp.float32)
    return total * (1.0 / channels)


def solution(mesh):
    placed = (P(("arrays", "tm"), "chan", None, None), P(("arrays", "tm")), P(("arrays", "chan")))
    return jax.shard_map(
        shards,
        mesh=mesh,
        in_specs=placed,
        out_specs=P(("arrays", "tm", "chan"), None, None),
        check_vma=False,
    )
```
